512 devices in a mesh: pages: 128 (over x, z, core), queries: 4 (over y).
Axes of the slice: x: 4, y: 4, z: 16, core: 2. Of those that a mesh axis runs over, the one named last changes fastest.
Arguments:
- page_states: bfloat16 [256, 768, 1536], P('pages', None, 'queries'), may hold values from -6 to 6
- projection: bfloat16 [1536, 128], P('queries'), may hold values from -0.59765625 to 0.59765625
- query_tokens: bfloat16 [8192, 32, 128], P(('pages', 'queries')), may hold values from -0.29882812 to 0.29882812
- candidates: int32 [8192, 16], P(('pages', 'queries')), may hold values from 0 to 255, all different within a row; in each aligned block of 16 rows (0 to 15, 16 to 31, ...) at most 2 rows name the same one
- patch_index: int32 [8192, 16, 32], P(('pages', 'queries')), may hold values from 0 to 767
- teacher_logits: float32 [8192, 16], P(('pages', 'queries')), may hold values from -10 to 10
- page_slot: int32 [256], replicated, may hold values from 0 to 255, each once
Outputs:
- grad_queries: float32 [8192, 32, 128], P(('pages', 'queries'))
- grad_projection: float32 [1536, 128], P('queries')
The draws below stay inside these ranges and needn't reach their ends.
Inputs may be any that keep to these rules, and one draw needn't show every extreme that they name: `candidates`: the 16 ids in one query's row differ. Among the 16 rows of one device no page id is listed more than 2 times, and in some device's rows one id is listed exactly 2 times. `page_slot`: each slot of 0 to 255 is taken by exactly one page id.
All inputs are finite; a program needn't handle non-finite values.
Results may differ from the reference program's by a relative error of at most 0.0052.
Values may be sent and summed in bfloat16 or wider, within the bound.
A program may use at most 64 MiB of HBM per device.

```python
import math
import jax
import jax.numpy as jnp
import numpy as np
from jax import lax

DIM = 128
HID = 1536
PATCH = 768
QT = 32
NC = 16
Q_DEV = 16
PAGES = 256
NQ = 8192
CAP = 2


def with_ends(array, key, smallest, largest):
    dims = array.shape
    spot = [jax.random.randint(jax.random.fold_in(key, axis), (), 0, dims[axis]) for axis in range(len(dims))]
    array = array.at[tuple(spot)].set(smallest)
    longest = dims.index(max(dims))
    spot[longest] = (spot[longest] + 1) % dims[longest]
    return array.at[tuple(spot)].set(largest)


def block_scale(rng, dims, pieces, smallest, high):
    factor_of = 1.0
    for axis_at, parts in pieces:
        heights = jax.random.uniform(jax.random.fold_in(jax.random.fold_in(rng, 6), axis_at), (parts,), jnp.float32, smallest / len(pieces), high / len(pieces))
        factor_of = factor_of * jnp.repeat(jnp.exp(heights), dims[axis_at] // parts).reshape((-1,) + (1,) * (len(dims) - 1 - axis_at))
    return factor_of


def routed_block(key, own, number, rows, number_of, top, limit, slope):
    order = jax.random.permutation(key, number_of)
    crowded, ordinary = load_shares(number_of, rows * top, limit, slope, True), load_shares(number_of, rows * top, limit, slope, False)
    places = jnp.arange(number_of)

    def named(lengths, rotation):
        used = int((lengths > 0).sum())
        fixed = max(1, used // 4)
        passed = fixed + (places - fixed + rotation * (used - fixed)) % max(1, number_of - fixed)
        return jnp.zeros((number_of,), jnp.int32).at[order[jnp.where(places < fixed, places, passed)]].set(jnp.asarray(lengths, jnp.int32))

    lengths = jnp.where(number % 4 == 0, named(crowded, number // 4), named(ordinary, number - number // 4 - 1))
    mixed = jax.random.permutation(jax.random.fold_in(own, 3), number_of)
    donor, taker = mixed[0:number_of // 2 * 2:2], mixed[1:number_of // 2 * 2:2]
    slack = jnp.minimum(lengths[donor] - 1, limit - lengths[taker]) // 2
    slack = jnp.where((donor == order[0]) | (taker == order[0]) | (lengths[taker] == 0), 0, jnp.maximum(slack, 0))
    passed = jax.random.randint(jax.random.fold_in(own, 4), (number_of // 2,), 0, 1 << 20) % (slack + 1)
    lengths = lengths.at[donor].add(-passed).at[taker].add(passed)
    labels = jnp.searchsorted(jnp.cumsum(lengths), jnp.arange(rows * top), side="right").astype(jnp.int32)
    listing = labels.reshape(top, rows).T
    listing = listing[jax.random.permutation(jax.random.fold_in(own, 1), rows)]
    rotation = jax.random.randint(jax.random.fold_in(own, 2), (rows, 1), 0, top)
    return jnp.take_along_axis(listing, (jnp.arange(top)[None, :] + rotation) % top, axis=1)


def load_shares(amount, total, most, lean, full):
    portions = [(1 << 20) // math.isqrt(grade ** lean) + 1 for grade in range(1, amount + 1)]
    largest = most if full else min(most, max(-(-total // amount), total * portions[0] // sum(portions)))
    least = 1 if total - largest >= amount - 1 else 0
    given, rest = [largest] + [least] * (amount - 1), total - largest - least * (amount - 1)
    while rest > 0:
        free = [i for i in range(1, amount) if given[i] < largest] or [i for i in range(1, amount) if given[i] < most]
        whole, remaining = sum([portions[i] for i in free]), rest
        for i in free:
            extra = min(most - given[i], max(1, remaining * portions[i] // whole), rest)
            given[i] = given[i] + extra
            rest = rest - extra
    return np.array(given)


def bell_draw(key, shape, scale, limit, split=(), dtype=jnp.bfloat16):
    drawn = jax.random.normal(key, shape, jnp.float32) * scale
    if len(split) > 0:
        drawn = block_scale(key, shape, split, -0.22, 0.18) * drawn
    return jnp.clip(drawn, min=-limit, max=limit).astype(dtype)


def setup_inputs(seed: int = 0) -> dict:
    key_list = jax.random.split(jax.random.key(seed), 8)
    page_states = bell_draw(key_list[0], (PAGES, PATCH, HID), 1.0, 6.0, ((0, 128), (2, 4)))
    projection = bell_draw(key_list[1], (HID, DIM), 0.1, 0.59765625, ((0, 4),))
    query_tokens = bell_draw(key_list[2], (NQ, QT, DIM), 0.05, 0.29882812, ((0, 512),))
    candidates_keys = jax.random.split(jax.random.fold_in(key_list[3], 1), NQ // Q_DEV)
    candidates_turns = jax.random.permutation(jax.random.fold_in(key_list[3], 3), NQ // Q_DEV)
    candidates = jax.vmap(lambda own, number: routed_block(jax.random.fold_in(key_list[3], 2), own, number, Q_DEV, PAGES, NC, CAP, 2))(candidates_keys, candidates_turns).reshape((NQ, NC))
    patch_index = with_ends(jax.random.randint(key_list[4], (NQ, NC, QT), 0, PATCH), jax.random.fold_in(key_list[4], 1), 0, PATCH - 1).astype(jnp.int32)
    teacher_logits = bell_draw(key_list[5], (NQ, NC), 3.0, 10.0, ((0, 512),), jnp.float32)
    page_slot = jax.random.permutation(key_list[6], PAGES).astype(jnp.int32)
    return {"page_states": page_states, "projection": projection, "query_tokens": query_tokens, "candidates": candidates, "patch_index": patch_index, "teacher_logits": teacher_logits, "page_slot": page_slot}


SOFTMAX_HEAT = 0.5
EPSILON = 1e-06

def unit_rows(values):
    inverse = lax.rsqrt(lax.optimization_barrier(jnp.sum(values * values, axis=-1, keepdims=True)) + EPSILON)
    return (values * inverse, inverse)

def reference(page_states, projection, query_tokens, candidates, patch_index, teacher_logits, page_slot):

    def project(states):
        return jnp.dot(states, projection, preferred_element_type=jnp.float32)
    embedded = lax.map(project, page_states)
    unit_embed32, inv_embed = unit_rows(embedded)
    unit_embed = unit_embed32.astype(jnp.bfloat16)
    unit_query32, inv_query = unit_rows(query_tokens.astype(jnp.float32))
    unit_query = unit_query32.astype(jnp.bfloat16)
    page_rows = page_slot[candidates].astype(jnp.int32)
    query_total, cand_count, tok_count = patch_index.shape
    embed_width = query_tokens.shape[2]
    block_rows = math.gcd(query_total, 256)
    block_count = query_total // block_rows

    def split_rows(values):
        return values.reshape((block_count, block_rows) + values.shape[1:])

    def block_step(running, block_items):
        query_bf, query_single_float, query_inv, slot_rows, patch_ids, teacher = block_items
        gathered = unit_embed[slot_rows[:, :, None], patch_ids]
        score_matrix = jnp.einsum('ntd,nctd->nc', query_bf.astype(jnp.float32), gathered.astype(jnp.float32))
        student_logits = jnp.exp(score_matrix / SOFTMAX_HEAT)
        student_logits = student_logits / lax.optimization_barrier(jnp.sum(student_logits, axis=1, keepdims=True))
        target_probs = jnp.exp(teacher)
        target_probs = target_probs / lax.optimization_barrier(jnp.sum(target_probs, axis=1, keepdims=True))
        weight_factor = ((student_logits - target_probs) / SOFTMAX_HEAT).astype(jnp.bfloat16)
        weight32 = weight_factor.astype(jnp.float32)
        grad_unit = jnp.einsum('nc,nctd->ntd', weight32, gathered.astype(jnp.float32))
        grad_query = (grad_unit - query_single_float * lax.optimization_barrier(jnp.sum(query_single_float * grad_unit, axis=-1, keepdims=True))) * query_inv
        weighted = weight32[:, :, None, None] * query_bf.astype(jnp.float32)[:, None, :, :]
        running = running.at[slot_rows[:, :, None], patch_ids].add(weighted)
        return (running, grad_query)
    start_grad = jnp.zeros(unit_embed32.shape, jnp.float32)
    grad_unit_embed, grad_blocks = lax.scan(block_step, start_grad, (split_rows(unit_query), split_rows(unit_query32), split_rows(inv_query), split_rows(page_rows), split_rows(patch_index), split_rows(teacher_logits)))
    grad_queries = grad_blocks.reshape(query_total, tok_count, embed_width)
    grad_embed = ((grad_unit_embed - unit_embed32 * lax.optimization_barrier(jnp.sum(unit_embed32 * grad_unit_embed, axis=-1, keepdims=True))) * inv_embed).astype(jnp.bfloat16)

    def accumulate(running, pair_items):
        states, gradient = pair_items
        return (running + jnp.dot(states.T, gradient, preferred_element_type=jnp.float32), None)
    start_proj = jnp.zeros(projection.shape, jnp.float32)
    grad_projection, unused = lax.scan(accumulate, start_proj, (page_states, grad_embed))
    return (grad_queries, grad_projection)
```

```python
import functools

import jax
import jax.numpy as jnp
from jax import lax
from jax.experimental import pallas as pl
from jax.experimental.pallas import tpu as pltpu
from jax.sharding import PartitionSpec as P

SOFTMAX_HEAT = 0.5
EPSILON = 1e-06
CAP = 2
X = 4
MESH = pl.DeviceIdType.MESH
VMEM = pl.BlockSpec(memory_space=pltpu.VMEM)
SUBS = 2


def unit_rows(values):
    inverse = lax.rsqrt(jnp.sum(values * values, axis=-1, keepdims=True) + EPSILON)
    return (values * inverse, inverse)


def place(zs):
    p = lax.axis_index("pages")
    return p // (2 * zs), lax.axis_index("queries"), (p // 2) % zs, p % 2


def dev(zs, x, y, z, c):
    return ((x * zs + z) * 2 + c, y)


def remote(src, dst, send, recv, to):
    return pltpu.make_async_remote_copy(
        src_ref=src, dst_ref=dst, send_sem=send, recv_sem=recv, device_id=to, device_id_type=MESH
    )


def greet(barrier, devices):
    for to in devices:
        pl.semaphore_signal(barrier, inc=1, device_id=to, device_id_type=MESH)
    pl.semaphore_wait(barrier, len(devices))


def gather_kernel(
    zs, ys, q, idx, nt, ep, qall, idxall, ntall, table, ef, rs,
    q_s, q_r, e_s, e_r, t_s, t_r, f_s, f_r, i_s, i_r, n_s, n_r,
):
    x, y, z, c = place(zs)
    at = functools.partial(dev, zs)
    rows = ef.shape[0]
    part = q.shape[0] // SUBS
    half = zs // 2
    plane = [(dx, dy) for dx in range(X) for dy in range(ys) if dx + dy > 0]
    greet(
        pltpu.get_barrier_semaphore(),
        [at(x, y, (z + d) % zs, c) for d in range(1, zs)]
        + [at((x + dx) % X, (y + dy) % ys, z, c) for dx, dy in plane]
        + [at(x, y, z, 1 - c)],
    )
    qall[z] = q[...]

    def ring(way, s, h, block):
        ref = qall.at[block, pl.ds(h * part, part)]
        k = 0 if way > 0 else 1
        return remote(ref, ref, q_s.at[k, s, h], q_r.at[k, s, h], at(x, y, (z + way + zs) % zs, c))

    def ring_parts(way, s):
        if s < half - 1:
            return range(SUBS)
        return range(SUBS // 2) if way > 0 else range(SUBS // 2, SUBS)

    def ring_send(s):
        for h in range(SUBS):
            for way in (1, -1):
                block = (z - way * s + zs) % zs
                if s > 0:
                    ring(way, s - 1, h, block).wait_recv()
                if h in ring_parts(way, s):
                    ring(way, s, h, block).start()

    ring_send(0)
    e_copies = []
    for d in range(1, ys):
        yd = (y + d) % ys
        src = ep.at[pl.ds(pl.multiple_of(yd * rows, 8), rows)]
        e_copies.append(remote(src, rs.at[d - 1], e_s.at[d - 1], e_r.at[d - 1], at(x, yd, z, c)))
        e_copies[-1].start()
    i_copies = []
    for d in range(1, zs):
        zd = (z + d) % zs
        to = at(x, y, zd, c)
        i_copies.append(remote(idx.at[zd], idxall.at[z], i_s.at[d - 1], i_r.at[d - 1], to))
        i_copies.append(remote(nt.at[zd], ntall.at[z], n_s.at[d - 1], n_r.at[d - 1], to))
        i_copies[-2].start()
        i_copies[-1].start()
    idxall[z] = idx[z]
    ntall[z] = nt[z]
    ring_send(1)
    ring_send(2)

    for copy in e_copies:
        copy.wait_recv()
    own = ep[pl.ds(pl.multiple_of(y * rows, 8), rows), :]
    for d in range(1, ys):
        own = own + rs[d - 1]
    ef[...] = own
    table[x, c, y] = unit_rows(own)[0].astype(jnp.bfloat16)
    t_copies = []
    mine = table.at[x, c, y]
    for i, (dx, dy) in enumerate(plane):
        to = at((x + dx) % X, (y + dy) % ys, z, c)
        t_copies.append(remote(mine, mine, t_s.at[i], t_r.at[i], to))
        t_copies[-1].start()
    f_copies = []

    def forward(i, xx, yy):
        ref = table.at[xx, c, yy]
        f_copies.append(remote(ref, ref, f_s.at[i], f_r.at[i], at(x, y, z, 1 - c)))
        f_copies[-1].start()

    forward(len(plane), x, y)
    s = 3
    for i, (dx, dy) in enumerate(plane):
        if i % 3 == 0 and s < half:
            ring_send(s)
            s += 1
        t_copies[i].wait_recv()
        forward(i, (x - dx + X) % X, (y - dy + ys) % ys)
    while s < half:
        ring_send(s)
        s += 1
    for way in (1, -1):
        for h in ring_parts(way, half - 1):
            ring(way, half - 1, h, (z - way * half + zs) % zs).wait_recv()
    for copy in f_copies + i_copies:
        copy.wait_recv()
    for s in range(half):
        for way in (1, -1):
            for h in ring_parts(way, s):
                ring(way, s, h, (z - way * s + zs) % zs).wait_send()
    for copy in e_copies + i_copies + t_copies + f_copies:
        copy.wait_send()


def pick_kernel(n_ref, table, idxt, qall, picked, scored):
    m = pl.program_id(0)
    toks, slots = idxt.shape[1:]
    rows = table.shape[1]
    lanes = lax.broadcasted_iota(jnp.int32, (toks, rows), 1)
    group = 8
    page = table[0]
    ids = idxt[0]
    for g in range(slots // group):
        hot = jnp.concatenate(
            [
                jnp.where(ids[:, s : s + 1] == lanes, 1.0, 0.0).astype(jnp.bfloat16)
                for s in range(g * group, (g + 1) * group)
            ],
            axis=0,
        )
        got = jnp.dot(hot, page, preferred_element_type=jnp.float32)
        picked[0, g * group * toks : (g + 1) * group * toks, :] = got.astype(jnp.bfloat16)
        for i in range(group):
            s = g * group + i
            query = qall[n_ref[m * slots + s]].astype(jnp.float32)
            scored[0, s : s + 1, :] = jnp.sum(
                got[i * toks : (i + 1) * toks] * query, axis=0, keepdims=True
            )


def total_kernel(zs, part, total, seen, s_s, s_r):
    x, y, z, c = place(zs)
    peers = [dev(zs, x, y, (z + d) % zs, c) for d in range(1, zs)]
    greet(pltpu.get_barrier_semaphore(), peers)
    copies = [
        remote(part, seen.at[i], s_s.at[i], s_r.at[i], to) for i, to in enumerate(peers)
    ]
    for copy in copies:
        copy.start()
    out = part[...]
    for i, copy in enumerate(copies):
        copy.wait_recv()
        out = out + seen[i]
    total[...] = out
    for copy in copies:
        copy.wait_send()


def spread_kernel(n_ref, w_ref, picked, idxl, wl, qall, gq, ge, qsel):
    m = pl.program_id(0)
    slots = n_ref.shape[0] // pl.num_programs(0)
    toks = qall.shape[1]
    rows = ge.shape[1]

    @pl.when(m == 0)
    def _():
        gq[...] = jnp.zeros_like(gq)

    for s in range(slots):
        n = n_ref[m * slots + s]
        qsel[s * toks : (s + 1) * toks, :] = qall[n]
        rows_of = picked[0, s * toks : (s + 1) * toks, :].astype(jnp.float32)
        gq[n] = gq[n] + w_ref[m * slots + s] * rows_of
    total = slots * toks
    width = 256
    ids = lax.broadcasted_iota(jnp.int32, (rows, width), 0)
    out = jnp.zeros((rows, qall.shape[2]), jnp.float32)
    for k in range(total // width):
        cut = slice(k * width, (k + 1) * width)
        hot = jnp.where(idxl[0, :, cut] == ids, wl[0, :, cut], 0.0).astype(jnp.bfloat16)
        out = out + jnp.dot(hot, qsel[cut, :], preferred_element_type=jnp.float32)
    ge[0] = out


def reduce_kernel(
    zs, ys, gq, ge, ef, gout, eout, rbuf, cbuf, sbuf, xbuf,
    g_s, g_r, c_s, c_r, t_s, t_r, y_s, y_r,
):
    x, y, z, c = place(zs)
    at = functools.partial(dev, zs)
    half = zs // 2
    part = gout.shape[0] // 2
    rows = ef.shape[0]
    plane = [(dx, dy) for dx in range(X) for dy in range(ys) if dx + dy > 0]
    greet(
        pltpu.get_barrier_semaphore(),
        [at(x, y, (z + 1) % zs, c), at(x, y, (z + zs - 1) % zs, c)]
        + [at((x + dx) % X, (y + dy) % ys, z, c) for dx, dy in plane]
        + [at(x, y, z, 1 - c)],
    )

    def first(way, h):
        return 0 if (h == 0) == (way > 0) else 1

    def ring(way, s, h):
        k = 0 if way > 0 else 1
        block = (z + way * (half - s) + zs) % zs
        cut = pl.ds(h * part, part)
        src = gq.at[block, cut] if s == first(way, h) else rbuf.at[k, s - 1, cut]
        return remote(
            src, rbuf.at[k, s, cut], g_s.at[k, s, h], g_r.at[k, s, h],
            at(x, y, (z + way + zs) % zs, c),
        )

    def ring_step(s):
        for h in range(2):
            for way in (1, -1):
                k = 0 if way > 0 else 1
                start = first(way, h)
                if s < start:
                    continue
                if s > start:
                    ring(way, s - 1, h).wait_recv()
                    block = (z + way * (half - s) + zs) % zs
                    cut = pl.ds(h * part, part)
                    rbuf[k, s - 1, cut] = rbuf[k, s - 1, cut] + gq[block, cut]
                ring(way, s, h).start()

    ring_step(0)
    c_copies = []
    for dx in range(X):
        xx = (x + dx) % X
        c_copies.append(
            remote(ge.at[xx, 1 - c], cbuf.at[xx], c_s.at[dx], c_r.at[dx], at(x, y, z, 1 - c))
        )
    for dx in list(range(1, X)) + [0]:
        c_copies[dx].start()
    ring_step(1)
    t_copies = {}
    for dx in list(range(1, X)) + [0]:
        xx = (x + dx) % X
        c_copies[dx].wait_recv()
        for dy in range(ys):
            yy = (y + dy) % ys
            cut = pl.ds(pl.multiple_of(yy * rows, 8), rows)
            both = ge[xx, c, cut] + cbuf[xx, cut]
            if dx + dy == 0:
                own = both
                continue
            i = plane.index((dx, dy))
            sbuf[i] = both.astype(jnp.bfloat16)
            to = at(xx, yy, z, c)
            t_copies[i] = remote(sbuf.at[i], xbuf.at[i], t_s.at[i], t_r.at[i], to)
            t_copies[i].start()
    ring_step(2)
    ring_step(3)
    ring_step(4)
    for i in range(len(plane)):
        t_copies[i].wait_recv()
        own = own + xbuf[i].astype(jnp.float32)
    unit, inverse = unit_rows(ef[...])
    grad = (own - unit * jnp.sum(unit * own, axis=-1, keepdims=True)) * inverse
    eout[y] = grad.astype(jnp.bfloat16)
    y_copies = []
    for d in range(1, ys):
        y_copies.append(
            remote(
                eout.at[y], eout.at[y], y_s.at[d - 1], y_r.at[d - 1], at(x, (y + d) % ys, z, c)
            )
        )
        y_copies[-1].start()
    for s in range(5, half):
        ring_step(s)
    out = gq[z]
    for k, way in ((0, 1), (1, -1)):
        for h in range(2):
            ring(way, half - 1, h).wait_recv()
        out = out + rbuf[k, half - 1]
    gout[...] = out
    for copy in y_copies:
        copy.wait_recv()
    for s in range(half):
        for way in (1, -1):
            for h in range(2):
                if s >= first(way, h):
                    ring(way, s, h).wait_send()
    for copy in c_copies + list(t_copies.values()) + y_copies:
        copy.wait_send()


def sum_kernel(
    zs, part, out, abuf, bsrc, bbuf, a_s, a_r, b_s, b_r, c_s, c_r, d_s, d_r
):
    x, y, z, c = place(zs)
    at = functools.partial(dev, zs)
    rows = part.shape[0] // (2 * X)
    owners = rows // 8
    plane = [(dx, dc) for dx in range(X) for dc in range(2) if dx + dc > 0]
    near = [at((x + dx) % X, y, z, (c + dc) % 2) for dx, dc in plane]
    far = [at(x, y, (z + d) % zs, c) for d in range(1, zs)]
    greet(pltpu.get_barrier_semaphore(), near + far)
    me = x * 2 + c

    def block(k):
        return pl.ds(pl.multiple_of(k * rows, 8), rows)

    a_copies = []
    for i, (dx, dc) in enumerate(plane):
        k = ((x + dx) % X) * 2 + (c + dc) % 2
        a_copies.append(remote(part.at[block(k)], abuf.at[i], a_s.at[i], a_r.at[i], near[i]))
        a_copies[-1].start()
    own = part[block(me), :]
    for i, copy in enumerate(a_copies):
        copy.wait_recv()
        own = own + abuf[i]
    bsrc[...] = own

    def tile(k):
        return pl.ds(pl.multiple_of(k * 8, 8), 8)

    def b_copy(k, i, to):
        return remote(bsrc.at[tile(k)], bbuf.at[i], b_s.at[k], b_r.at[i], to)

    for k in range(owners):
        @pl.when(z != k)
        def _():
            b_copy(k, z, at(x, y, k, c)).start()

    my_tile = pl.ds(pl.multiple_of(me * rows + z * 8, 8), 8)

    def c_copy(i, zd):
        return remote(out.at[my_tile], out.at[my_tile], c_s.at[i], c_r.at[z], at(x, y, zd, c))

    @pl.when(z < owners)
    def _():
        total = bsrc[tile(z), :]
        for d in range(1, zs):
            i = (z + d) % zs
            b_copy(0, i, at(x, y, i, c)).wait_recv()
            total = total + bbuf[i]
        out[my_tile, :] = total
        for d in range(1, zs):
            c_copy(d - 1, (z + d) % zs).start()

    for k in range(owners):
        @pl.when(z != k)
        def _():
            got = out.at[pl.ds(pl.multiple_of(me * rows + k * 8, 8), 8)]
            remote(got, got, c_s.at[0], c_r.at[k], at(x, y, k, c)).wait_recv()

    d_copies = []
    for i in range(len(plane)):
        ref = out.at[block(me)]
        d_copies.append(remote(ref, ref, d_s.at[i], d_r.at[i], near[i]))
        d_copies[-1].start()
    for copy in d_copies:
        copy.wait_recv()
    for copy in a_copies + d_copies:
        copy.wait_send()
    for k in range(owners):
        @pl.when(z != k)
        def _():
            b_copy(k, z, at(x, y, k, c)).wait_send()

    @pl.when(z < owners)
    def _():
        for d in range(1, zs):
            c_copy(d - 1, (z + d) % zs).wait_send()


def dma(*shape):
    return pltpu.SemaphoreType.DMA(shape)


def talk(number):
    return pltpu.CompilerParams(
        collective_id=number, has_side_effects=True, vmem_limit_bytes=48 << 20
    )


def body(page_states, projection, query_tokens, candidates, patch_index, teacher_logits, page_slot):
    ys = lax.axis_size("queries")
    zs = lax.axis_size("pages") // (2 * X)
    held, patches, share = page_states.shape
    width = projection.shape[1]
    nq, nc, toks = patch_index.shape
    pages = page_slot.shape[0]
    pairs = nq * nc
    chip = 2 * held
    slab = X * chip
    slots = slab * CAP
    rows = held * patches // ys
    f32, bf16, i32 = jnp.float32, jnp.bfloat16, jnp.int32
    S = jax.ShapeDtypeStruct
    plane = X * ys - 1
    half = zs // 2

    states = page_states.reshape(held * patches, share)
    partial = jnp.dot(states, projection, preferred_element_type=f32)
    unit_query32, inv_query = unit_rows(query_tokens.astype(f32))
    unit_query = unit_query32.astype(bf16)

    flat = candidates.reshape(pairs)
    ids = jnp.arange(pages, dtype=i32)
    row = jnp.sum(jnp.where(flat[:, None] == ids[None, :], page_slot[None, :], 0), axis=1)
    before = jnp.arange(pairs)[None, :] < jnp.arange(pairs)[:, None]
    arrival = jnp.sum(((row[:, None] == row[None, :]) & before).astype(i32), axis=1)
    target = (
        ((row // chip) % zs * slab + row // (chip * zs) * chip + row % chip) * CAP + arrival
    )
    hot = target[None, :] == jnp.arange(zs * slots, dtype=i32)[:, None]
    number = jnp.sum(jnp.where(hot, jnp.arange(pairs, dtype=i32)[None, :] // nc + 1, 0), axis=1) - 1
    probs = jnp.exp(teacher_logits)
    probs = probs / jnp.sum(probs, axis=1, keepdims=True)
    teach = jnp.sum(jnp.where(hot, probs.reshape(1, pairs), 0.0), axis=1)
    flat_index = patch_index.reshape(pairs, toks)
    digits = jnp.concatenate([flat_index // 32, flat_index % 32], axis=1).astype(bf16)
    digits = jnp.dot(hot.astype(bf16), digits, preferred_element_type=f32)
    index = (digits[:, :toks] * 32 + digits[:, toks:]).astype(i32)
    index = jnp.where(number[:, None] >= 0, index, -1)
    index = index.reshape(zs, slots * toks // 128, 128)
    nt = jnp.concatenate(
        [
            number.astype(f32).reshape(zs, slots),
            teach.reshape(zs, slots),
            jnp.zeros((zs, 128 - 2 * slots), f32),
        ],
        axis=1,
    ).reshape(zs, 1, 128)

    qall, idxall, ntall, table, ef = pl.pallas_call(
        functools.partial(gather_kernel, zs, ys),
        out_shape=(
            S((zs, nq * toks, width), bf16),
            S(index.shape, i32),
            S(nt.shape, f32),
            S((X, 2, ys, rows, width), bf16),
            S((rows, width), f32),
        ),
        in_specs=[VMEM] * 4,
        out_specs=(VMEM,) * 5,
        scratch_shapes=[
            pltpu.VMEM((ys - 1, rows, width), f32),
            dma(2, half, SUBS), dma(2, half, SUBS),
            dma(ys - 1), dma(ys - 1),
            dma(plane), dma(plane),
            dma(plane + 1), dma(plane + 1),
            dma(zs - 1), dma(zs - 1),
            dma(zs - 1), dma(zs - 1),
        ],
        compiler_params=talk(0),
        name="gather",
    )(unit_query.reshape(nq * toks, width), index, nt, partial)

    per_page = zs * CAP
    idx4 = idxall.reshape(zs, slab, CAP, toks)
    idxt = idx4.transpose(1, 3, 0, 2).reshape(slab, toks, per_page)
    idxl = idx4.transpose(1, 0, 2, 3).reshape(slab, 1, per_page * toks)
    num = ntall[:, 0, :slots].astype(i32).reshape(zs, slab, CAP).transpose(1, 0, 2)
    teach = ntall[:, 0, slots : 2 * slots].reshape(zs, slab, CAP).transpose(1, 0, 2)
    valid = num >= 0
    where = jnp.maximum(num, 0) + nq * jnp.arange(zs, dtype=i32)[None, :, None]
    where = where.reshape(slab * per_page)
    qall = qall.reshape(zs * nq, toks, width)
    table = table.reshape(slab, patches, width)
    whole = pl.BlockSpec((zs * nq, toks, width), lambda m, *_: (0, 0, 0))

    def one(*shape):
        return pl.BlockSpec((1,) + shape, lambda m, *_: (m, 0, 0))

    picked, scored = pl.pallas_call(
        pick_kernel,
        out_shape=(S((slab, per_page * toks, width), bf16), S((slab, per_page, width), f32)),
        grid_spec=pltpu.PrefetchScalarGridSpec(
            num_scalar_prefetch=1,
            grid=(slab,),
            in_specs=[one(patches, width), one(toks, per_page), whole],
            out_specs=(one(per_page * toks, width), one(per_page, width)),
        ),
        compiler_params=pltpu.CompilerParams(vmem_limit_bytes=48 << 20),
        name="pick",
    )(where, table, idxt, qall)

    scores = jnp.sum(scored, axis=-1).reshape(slab, zs, CAP)
    lifted = jnp.where(valid, jnp.exp(scores / SOFTMAX_HEAT), 0.0)
    is_n = num[..., None] == jnp.arange(nq, dtype=i32)
    part = jnp.sum(jnp.where(is_n, lifted[..., None], 0.0), axis=(0, 2))
    total = pl.pallas_call(
        functools.partial(total_kernel, zs),
        out_shape=S((zs * nq // 128, 128), f32),
        in_specs=[VMEM],
        out_specs=VMEM,
        scratch_shapes=[
            pltpu.VMEM((zs - 1, zs * nq // 128, 128), f32), dma(zs - 1), dma(zs - 1),
        ],
        compiler_params=talk(1),
        name="total",
    )(part.reshape(zs * nq // 128, 128)).reshape(1, zs, 1, nq)
    mine = jnp.sum(jnp.where(is_n, total, 0.0), axis=-1)
    weight = jnp.where(
        valid, (lifted / jnp.where(valid, mine, 1.0) - teach) / SOFTMAX_HEAT, 0.0
    ).astype(bf16).astype(f32)
    flat_weight = weight.reshape(slab * per_page)
    wide = jnp.broadcast_to(
        weight.reshape(slab, 1, per_page, 1), (slab, 1, per_page, toks)
    ).reshape(slab, 1, per_page * toks)

    gq, ge = pl.pallas_call(
        spread_kernel,
        out_shape=(S((zs * nq, toks, width), f32), S((slab, patches, width), f32)),
        grid_spec=pltpu.PrefetchScalarGridSpec(
            num_scalar_prefetch=2,
            grid=(slab,),
            in_specs=[
                one(per_page * toks, width), one(1, per_page * toks), one(1, per_page * toks),
                whole,
            ],
            out_specs=(whole, one(patches, width)),
            scratch_shapes=[pltpu.VMEM((per_page * toks, width), bf16)],
        ),
        compiler_params=pltpu.CompilerParams(vmem_limit_bytes=48 << 20),
        name="spread",
    )(where, flat_weight, picked, idxl, wide, qall)

    gout, eout = pl.pallas_call(
        functools.partial(reduce_kernel, zs, ys),
        out_shape=(S((nq * toks, width), f32), S((ys, rows, width), bf16)),
        in_specs=[VMEM] * 3,
        out_specs=(VMEM,) * 2,
        scratch_shapes=[
            pltpu.VMEM((2, half, nq * toks, width), f32),
            pltpu.VMEM((X, held * patches, width), f32),
            pltpu.VMEM((plane, rows, width), bf16),
            pltpu.VMEM((plane, rows, width), bf16),
            dma(2, half, 2), dma(2, half, 2),
            dma(X), dma(X),
            dma(plane), dma(plane),
            dma(ys - 1), dma(ys - 1),
        ],
        compiler_params=talk(2),
        name="reduce",
    )(gq.reshape(zs, nq * toks, width), ge.reshape(X, 2, held * patches, width), ef)

    grad_unit = gout.reshape(nq, toks, width)
    grad_queries = (
        grad_unit - unit_query32 * jnp.sum(unit_query32 * grad_unit, axis=-1, keepdims=True)
    ) * inv_query
    grad_part = lax.dot_general(
        states, eout.reshape(held * patches, width), (((0,), (0,)), ((), ())),
        preferred_element_type=f32,
    )
    near = 2 * X - 1
    block = share // (2 * X)
    grad_projection = pl.pallas_call(
        functools.partial(sum_kernel, zs),
        out_shape=S((share, width), f32),
        in_specs=[VMEM],
        out_specs=VMEM,
        scratch_shapes=[
            pltpu.VMEM((near, block, width), f32),
            pltpu.VMEM((block, width), f32),
            pltpu.VMEM((zs, 8, width), f32),
            dma(near), dma(near),
            dma(block // 8), dma(zs),
            dma(zs), dma(zs),
            dma(near), dma(near),
        ],
        compiler_params=talk(3),
        name="sum",
    )(grad_part)
    return (grad_queries, grad_projection)


def solution(mesh):
    placed = (
        P("pages", None, "queries"),
        P("queries", None),
        P(("pages", "queries"), None, None),
        P(("pages", "queries"), None),
        P(("pages", "queries"), None, None),
        P(("pages", "queries"), None),
        P(),
    )
    return jax.shard_map(
        body,
        mesh=mesh,
        in_specs=placed,
        out_specs=(P(("pages", "queries"), None, None), P("queries", None)),
        check_vma=False,
    )
```

```python
import functools

import jax
import jax.numpy as jnp
from jax import lax
from jax.experimental import pallas as pl
from jax.experimental.pallas import tpu as pltpu
from jax.sharding import PartitionSpec as P

SOFTMAX_HEAT = 0.5
EPSILON = 1e-06
CAP = 2
X = 4
LANES = 128
SUBS = 4
MESH = pl.DeviceIdType.MESH
VMEM = pl.BlockSpec(memory_space=pltpu.VMEM)
F32, BF16, I32 = jnp.float32, jnp.bfloat16, jnp.int32


def unit_rows(values):
    inverse = lax.rsqrt(jnp.sum(values * values, axis=-1, keepdims=True) + EPSILON)
    return (values * inverse, inverse)


def iota(shape, axis):
    return lax.broadcasted_iota(I32, shape, axis)


def remote(src, dst, send, recv, to):
    return pltpu.make_async_remote_copy(
        src_ref=src, dst_ref=dst, send_sem=send, recv_sem=recv, device_id=to, device_id_type=MESH
    )


def kernel(
    zs, ys,
    states, proj, qraw, idx, nt,
    gq_out, gp_out,
    qall, idxall, ntall, ep, rs, ef, table, kge, kg, wge, wg, picked, qsel, sc, sm, nv, nsm,
    zpart, zseen, ge, gbuf, rbuf, cbuf, sbuf, xbuf, eout, part, abuf, bsrc, bbuf,
    q_s, q_r, e_s, e_r, t_s, t_r, f_s, f_r, i_s, i_r, n_s, n_r, m_s, z_s, z_r,
    g_s, g_r, c_s, c_r, p_s, p_r, y_s, y_r, a_s, a_r, b_s, b_r, o_s, o_r, d_s, d_r,
):
    p = lax.axis_index("pages")
    x, y, z, c = p // (2 * zs), lax.axis_index("queries"), (p // 2) % zs, p % 2

    def at(x_, y_, z_, c_):
        return ((x_ * zs + z_) * 2 + c_, y_)

    def xm(d):
        return (x + d + X) % X

    def ym(d):
        return (y + d + ys) % ys

    def zm(d):
        return (z + d + 2 * zs) % zs

    rows, width = ef.shape
    queries, toks, _ = qraw.shape
    toks_q = queries * toks
    slab = kge.shape[0]
    patches = table.shape[3] * ys // 2
    blocks = ys // 2
    half = zs // 2
    plane = [(dx, dy) for dx in range(X) for dy in range(ys) if dx + dy > 0]
    near_by = [(dx, dc) for dx in range(X) for dc in range(2) if dx + dc > 0]

    barrier = pltpu.get_barrier_semaphore()
    peers = [at(x, y, zm(d), c) for d in range(1, zs)]
    peers += [at(xm(dx), ym(dy), z, c) for dx, dy in plane]
    peers += [at(xm(dx), y, z, 1 - c) for dx in range(X)]
    for to in peers:
        pl.semaphore_signal(barrier, inc=1, device_id=to, device_id_type=MESH)

    qall[z] = unit_rows(qraw[...].astype(F32))[0].astype(BF16)
    ep[...] = jnp.dot(states[...], proj[...], preferred_element_type=F32)
    idxall[z] = idx[z]
    ntall[z] = nt[z]
    sm[...] = jnp.zeros_like(sm)
    pl.semaphore_wait(barrier, len(peers))

    size = queries // SUBS

    def ring(way, s, h, block):
        ref = qall.at[block, pl.ds(h * size, size)]
        k = 0 if way > 0 else 1
        return remote(ref, ref, q_s.at[k, s, h], q_r.at[k, s, h], at(x, y, zm(way), c))

    def ring_parts(way, s):
        if s < half - 1:
            return range(SUBS)
        return range(SUBS // 2) if way > 0 else range(SUBS // 2, SUBS)

    def ring_send(s):
        for h in range(SUBS):
            for way in (1, -1):
                block = zm(-way * s)
                if s > 0:
                    ring(way, s - 1, h, block).wait_recv()
                if h in ring_parts(way, s):
                    ring(way, s, h, block).start()

    ring_send(0)
    e_copies = []
    for d in range(1, ys):
        src = ep.at[pl.ds(pl.multiple_of(ym(d) * rows, 8), rows)]
        to = at(x, ym(d), z, c)
        e_copies.append(remote(src, rs.at[d - 1], e_s.at[d - 1], e_r.at[d - 1], to))
        e_copies[-1].start()
    i_copies = []
    for d in range(1, zs):
        to = at(x, y, zm(d), c)
        for src, dst, s_sem, r_sem in ((idx, idxall, i_s, i_r), (nt, ntall, n_s, n_r)):
            copy = remote(src.at[zm(d)], dst.at[z], s_sem.at[d - 1], r_sem.at[d - 1], to)
            copy.start()
            i_copies.append(copy)
    ring_send(1)
    ring_send(2)

    for copy in e_copies:
        copy.wait_recv()
    own = ep[pl.ds(pl.multiple_of(y * rows, 8), rows), :]
    for d in range(1, ys):
        own = own + rs[d - 1]
    ef[...] = own
    table[x, c, y] = unit_rows(own)[0].astype(BF16)
    mine = table.at[x, c, y]
    t_copies = []
    for i, (dx, dy) in enumerate(plane):
        to = at(xm(dx), ym(dy), z, c)
        t_copies.append(remote(mine, mine, t_s.at[i], t_r.at[i], to))
        t_copies[-1].start()

    def sibling(dx, dy, core):
        i = dx * ys + dy
        ref = table.at[xm(-dx), core, ym(-dy)]
        return remote(ref, ref, f_s.at[i], f_r.at[i], at(x, y, z, 1 - c))

    def forward(dx):
        for dy in range(ys):
            if dx + dy > 0:
                i = plane.index((dx, dy))
                ref = table.at[xm(-dx), c, ym(-dy)]
                remote(ref, ref, t_s.at[i], t_r.at[i], at(x, y, z, 1 - c)).wait_recv()
            sibling(dx, dy, c).start()

    ring_send(3)

    for copy in i_copies:
        copy.wait_recv()
    lane8 = iota((8, LANES), 1)
    for j in range(zs // 2):
        a, b = ((idxall[i] & 1023) - 1 for i in (2 * j, 2 * j + 1))
        kge[0:8, j, :] = jnp.where(lane8 < 64, a, pltpu.roll(b, 64, 1))
        kge[8:16, j, :] = jnp.where(lane8 < 64, pltpu.roll(a, 64, 1), b)
    for s in range(zs):
        nv[s : s + 1, :] = ntall[s]
    lane = iota((zs, LANES), 1)
    number = nv[...]
    valid = (lane < CAP * slab) & (number >= 0)
    teach = pltpu.roll(number, LANES - CAP * slab, 1)
    scalars = pltpu.make_async_copy(idxall, nsm, m_s)
    scalars.start()
    wide = slab * CAP * toks
    lanes = iota((LANES, wide), 1)
    sub = iota((LANES, wide), 0)
    spread = (sub < CAP * slab) & ((sub & (slab - 1)) == (lanes >> 6))
    spread = spread & ((sub >> 4) == ((lanes >> 5) & 1))
    spread = jnp.where(spread, 1.0, 0.0).astype(BF16)
    keys = jnp.dot(
        jnp.where(valid, number, -64.0).astype(BF16), spread, preferred_element_type=F32
    )
    keys = keys.astype(I32) * toks + (iota((zs, wide), 1) & (toks - 1))
    for j in range(wide // LANES):
        kg[:, j, :] = keys[:, j * LANES : (j + 1) * LANES]
    scalars.wait()

    ring_send(4)
    forward(0)
    ring_send(5)
    ring_send(6)
    ring_send(7)
    forward(1)
    for way in (1, -1):
        for h in ring_parts(way, half - 1):
            ring(way, half - 1, h, zm(-way * half)).wait_recv()

    def pick_page(m):
        page = table[m // 4, (m // 2) % 2, pl.ds(blocks * (m % 2), blocks)]
        page = page.reshape(patches, width)
        cols = kge[m].T
        ids = iota((LANES, patches), 1)
        for g in range(zs // 4):
            hot = jnp.concatenate(
                [
                    jnp.where(cols[:, j : j + 1] == ids, 1.0, 0.0).astype(BF16)
                    for j in (2 * g, 2 * g + 1)
                ],
                axis=0,
            )
            got = jnp.dot(hot, page, preferred_element_type=F32)
            picked[m, g * 256 : (g + 1) * 256, :] = got.astype(BF16)
            for i in range(8):
                s = g * 8 + i
                src, k = s // CAP, s % CAP
                query = qall[src, nsm[src, m % 8, m // 8 * (CAP * toks) + k * toks] >> 10]
                qsel[m, s * toks : (s + 1) * toks, :] = query
                sc[k, src : src + 1, :] = jnp.sum(
                    got[i * toks : (i + 1) * toks] * query.astype(F32), axis=0, keepdims=True
                )
        for k in range(CAP):
            col = jnp.sum(sc[k], axis=1, keepdims=True)
            sm[...] = jnp.where(lane == k * slab + m, col, sm[...])

    for dx in range(X):
        if 0 < dx < X - 1:
            forward(dx + 1)
        for dy in range(ys):
            sibling(dx, dy, 1 - c).wait_recv()

        @pl.loop(0, 4)
        def _(i):
            pick_page(xm(-dx) * 4 + i)

    lifted = jnp.where(valid, jnp.exp(sm[...] / SOFTMAX_HEAT), 0.0)
    wide_sum = jnp.zeros((zs, LANES), F32)
    for n in range(16):
        col = jnp.sum(jnp.where(number == n, lifted, 0.0), axis=1, keepdims=True)
        wide_sum = jnp.where((lane & 15) == n, col, wide_sum)
    diagonal = (lane >> 4) == (iota((zs, LANES), 0) & 7)
    wide_sum = jnp.where(diagonal, wide_sum, 0.0)
    for r in range(zs // 8):
        zpart[r : r + 1, :] = jnp.sum(wide_sum[8 * r : 8 * r + 8], axis=0, keepdims=True)
    z_copies = []
    for d in range(1, zs):
        to = at(x, y, zm(d), c)
        z_copies.append(remote(zpart, zseen.at[d - 1], z_s.at[d - 1], z_r.at[d - 1], to))
        z_copies[-1].start()
    total = zpart[...]
    for d in range(1, zs):
        z_copies[d - 1].wait_recv()
        total = total + zseen[d - 1]
    total = jnp.concatenate(
        [jnp.broadcast_to(total[r : r + 1], (8, LANES)) for r in range(zs // 8)], axis=0
    )
    total = jnp.where(diagonal, total, 0.0)
    denom = jnp.ones((zs, LANES), F32)
    for n in range(16):
        col = jnp.sum(jnp.where((lane & 15) == n, total, 0.0), axis=1, keepdims=True)
        denom = jnp.where(valid & (number == n), col, denom)
    weight = jnp.where(valid, (lifted / denom - teach) / SOFTMAX_HEAT, 0.0)
    wide_w = jnp.dot(weight.astype(BF16), spread, preferred_element_type=F32)
    for j in range(wide // LANES):
        wg[:, j, :] = wide_w[:, j * LANES : (j + 1) * LANES]
    turned = weight.T
    wide_w = jnp.zeros((slab, zs * CAP * toks), F32)
    lanes = iota((zs, zs * CAP * toks), 1)
    sub = iota((zs, zs * CAP * toks), 0)
    for k in range(CAP):
        expand = (sub == (lanes >> 6)) & (((lanes >> 5) & 1) == k)
        expand = jnp.where(expand, 1.0, 0.0).astype(BF16)
        wide_w = wide_w + jnp.dot(
            turned[k * slab : (k + 1) * slab].astype(BF16), expand, preferred_element_type=F32
        )
    for j in range(zs * CAP * toks // LANES):
        wge[:, j, :] = wide_w[:, j * LANES : (j + 1) * LANES]

    def hot_pair(key, scale, a, j, ids):
        return jnp.concatenate(
            [
                jnp.where(
                    key[a, pl.ds(i, 1), :] == ids, scale[a, pl.ds(i, 1), :], 0.0
                ).astype(BF16)
                for i in (2 * j, 2 * j + 1)
            ],
            axis=1,
        )

    def query_block(src):
        out = jnp.zeros((toks_q, width), F32)
        ids = iota((toks_q, LANES), 0)
        per = CAP * toks
        first = pl.multiple_of(src * per, per)
        for j in range(wide // 256):
            rows_of = jnp.concatenate(
                [picked[m, pl.ds(first, per), :] for m in range(4 * j, 4 * j + 4)], axis=0
            )
            out = out + jnp.dot(
                hot_pair(kg, wg, src, j, ids), rows_of, preferred_element_type=F32
            )
        gbuf[src] = out

    def page_block(xx, cc, l):
        m = xx * 4 + cc * 2 + l
        out = jnp.zeros((patches, width), F32)
        ids = iota((patches, LANES), 0)
        for j in range(zs * CAP * toks // 256):
            out = out + jnp.dot(
                hot_pair(kge, wge, m, j, ids), qsel[m, j * 256 : (j + 1) * 256, :],
                preferred_element_type=F32,
            )
        ge[xx, cc, l * patches : (l + 1) * patches, :] = out

    part_rows = toks_q // 2

    def gring(way, s, h, begin=False):
        k = 0 if way > 0 else 1
        cut = pl.ds(h * part_rows, part_rows)
        src = gbuf.at[zm(way * (half - s)), cut] if begin else rbuf.at[k, s - 1, cut]
        return remote(
            src, rbuf.at[k, s, cut], g_s.at[k, s, h], g_r.at[k, s, h], at(x, y, zm(way), c)
        )

    def begins(way, h):
        return 0 if (h == 0) == (way > 0) else 1

    def gstep(s):
        if isinstance(s, int) and s == 0:
            query_block(zm(half))
        else:
            query_block(zm(half - s))
            query_block(zm(s - half))
        for h in range(2):
            for way in (1, -1):
                k = 0 if way > 0 else 1
                begin = isinstance(s, int) and s == begins(way, h)
                if isinstance(s, int) and s < begins(way, h):
                    continue
                if not begin:
                    cut = pl.ds(h * part_rows, part_rows)
                    early = isinstance(s, int) and s - 1 == begins(way, h)
                    gring(way, s - 1, h, early).wait_recv()
                    rbuf[k, s - 1, cut] = rbuf[k, s - 1, cut] + gbuf[zm(way * (half - s)), cut]
                gring(way, s, h, begin).start()

    gstep(0)

    def to_sibling(xx):
        return remote(
            ge.at[xx, 1 - c], cbuf.at[xx], c_s.at[xx], c_r.at[xx], at(x, y, z, 1 - c)
        )

    @pl.loop(1, X + 1)
    def _(d):
        for l in range(2):
            page_block(xm(d), 1 - c, l)
        to_sibling(xm(d)).start()

    gstep(1)

    def to_plane(i, xx, yy):
        return remote(sbuf.at[i], xbuf.at[i], p_s.at[i], p_r.at[i], at(xx, yy, z, c))

    @pl.loop(1, X + 1)
    def _(d):
        xx = xm(d)
        for l in range(2):
            page_block(xx, c, l)
        to_sibling(xx).wait_recv()
        for dy in range(ys):
            cut = pl.ds(pl.multiple_of(ym(dy) * rows, 8), rows)
            both = ge[xx, c, cut, :] + cbuf[xx, cut, :]
            i = (d % X) * ys + dy
            sbuf[i] = both.astype(BF16)
            if dy == 0:

                @pl.when(d < X)
                def _():
                    to_plane(i, xx, ym(dy)).start()
            else:
                to_plane(i, xx, ym(dy)).start()

    @pl.loop(2, 5)
    def _(s):
        gstep(s)

    cut = pl.ds(pl.multiple_of(y * rows, 8), rows)
    own = ge[x, c, cut, :] + cbuf[x, cut, :]
    for dx, dy in plane:
        i = dx * ys + dy
        to_plane(i, xm(dx), ym(dy)).wait_recv()
        own = own + xbuf[i].astype(F32)
    unit, inverse = unit_rows(ef[...])
    grad = (own - unit * jnp.sum(unit * own, axis=-1, keepdims=True)) * inverse
    eout[y] = grad.astype(BF16)
    y_copies = []
    for d in range(1, ys):
        to = at(x, ym(d), z, c)
        y_copies.append(remote(eout.at[y], eout.at[y], y_s.at[d - 1], y_r.at[d - 1], to))
        y_copies[-1].start()
    gstep(5)
    for copy in y_copies:
        copy.wait_recv()
    part[...] = lax.dot_general(
        eout[...].reshape(ys * rows, width), states[...], (((0,), (0,)), ((), ())),
        preferred_element_type=F32,
    ).T

    share = part.shape[0] // (2 * X)
    owners = share // 8
    near = [at(xm(dx), y, z, (c + dc) % 2) for dx, dc in near_by]

    def block(k):
        return pl.ds(pl.multiple_of(k * share, 8), share)

    def tile(k):
        return pl.ds(pl.multiple_of(k * 8, 8), 8)

    me = x * 2 + c
    a_copies = []
    for i, (dx, dc) in enumerate(near_by):
        k = xm(dx) * 2 + (c + dc) % 2
        a_copies.append(remote(part.at[block(k)], abuf.at[i], a_s.at[i], a_r.at[i], near[i]))
        a_copies[-1].start()
    gstep(6)
    own = part[block(me), :]
    for i, copy in enumerate(a_copies):
        copy.wait_recv()
        own = own + abuf[i]
    bsrc[...] = own

    def b_copy(k, i, to):
        return remote(bsrc.at[tile(k)], bbuf.at[i], b_s.at[k], b_r.at[i], to)

    for k in range(owners):

        @pl.when(z != k)
        def _():
            b_copy(k, z, at(x, y, k, c)).start()

    gstep(7)
    query_block(z)
    for k, way in ((0, 1), (1, -1)):
        for h in range(2):
            gring(way, half - 1, h).wait_recv()
    unit, inverse = unit_rows(qraw[...].reshape(toks_q, width).astype(F32))

    my_tile = pl.ds(pl.multiple_of(me * share + z * 8, 8), 8)

    def o_copy(i, to):
        return remote(gp_out.at[my_tile], gp_out.at[my_tile], o_s.at[i], o_r.at[z], to)

    @pl.when(z < owners)
    def _():
        total = bsrc[tile(z), :]
        for d in range(1, zs):
            i = zm(d)
            b_copy(0, i, at(x, y, i, c)).wait_recv()
            total = total + bbuf[i]
        gp_out[my_tile, :] = total
        for d in range(1, zs):
            o_copy(d - 1, at(x, y, zm(d), c)).start()

    own = gbuf[z] + rbuf[0, half - 1] + rbuf[1, half - 1]
    gq_out[...] = (own - unit * jnp.sum(unit * own, axis=-1, keepdims=True)) * inverse

    for k in range(owners):

        @pl.when(z != k)
        def _():
            got = gp_out.at[pl.ds(pl.multiple_of(me * share + k * 8, 8), 8)]
            remote(got, got, o_s.at[0], o_r.at[k], at(x, y, k, c)).wait_recv()

    d_copies = []
    for i in range(len(near_by)):
        ref = gp_out.at[block(me)]
        d_copies.append(remote(ref, ref, d_s.at[i], d_r.at[i], near[i]))
        d_copies[-1].start()
    for copy in d_copies:
        copy.wait_recv()

    for s in range(half):
        for way in (1, -1):
            for h in ring_parts(way, s):
                ring(way, s, h, zm(-way * s)).wait_send()
            for h in range(2):
                if s >= begins(way, h):
                    gring(way, s, h, s == begins(way, h)).wait_send()
    for dx in range(X):
        for dy in range(ys):
            sibling(dx, dy, c).wait_send()
            if dx + dy > 0:
                to_plane(dx * ys + dy, xm(dx), ym(dy)).wait_send()
        to_sibling(xm(dx)).wait_send()
    for copy in e_copies + i_copies + t_copies + z_copies + y_copies + a_copies + d_copies:
        copy.wait_send()
    for k in range(owners):

        @pl.when(z != k)
        def _():
            b_copy(k, z, at(x, y, k, c)).wait_send()

    @pl.when(z < owners)
    def _():
        for d in range(1, zs):
            o_copy(d - 1, at(x, y, zm(d), c)).wait_send()


def body(page_states, projection, query_tokens, candidates, patch_index, teacher_logits, page_slot):
    ys = lax.axis_size("queries")
    zs = lax.axis_size("pages") // (2 * X)
    held, patches, share = page_states.shape
    width = projection.shape[1]
    nq, nc, toks = patch_index.shape
    pages = page_slot.shape[0]
    pairs = nq * nc
    chip = 2 * held
    slab = X * chip
    slots = slab * CAP
    rows = held * patches // ys
    half = zs // 2
    per_page = zs * CAP * toks
    near = 2 * X - 1
    block = share // (2 * X)
    S = jax.ShapeDtypeStruct
    V = pltpu.VMEM

    flat = candidates.reshape(pairs)
    ids = jnp.arange(pages, dtype=I32)
    row = jnp.sum(jnp.where(flat[:, None] == ids[None, :], page_slot[None, :], 0), axis=1)
    before = jnp.arange(pairs)[None, :] < jnp.arange(pairs)[:, None]
    arrival = jnp.sum(((row[:, None] == row[None, :]) & before).astype(I32), axis=1)
    owner = (row // chip) % zs
    m = row // (chip * zs) * chip + row % chip
    all_slots = jnp.arange(zs * slots, dtype=I32)[:, None]
    hot = (owner * slots + m % 8 * (2 * CAP) + m // 8 * CAP + arrival)[None, :] == all_slots
    hot2 = (owner * slots + arrival * slab + m)[None, :] == all_slots
    numbers = jnp.arange(pairs, dtype=I32)[None, :] // nc + 1
    number = jnp.sum(jnp.where(hot2, numbers, 0), axis=1) - 1
    probs = jnp.exp(teacher_logits)
    probs = probs / jnp.sum(probs, axis=1, keepdims=True)
    teach = jnp.sum(jnp.where(hot2, probs.reshape(1, pairs), 0.0), axis=1)
    flat_index = patch_index.reshape(pairs, toks) + 1
    asker = jnp.broadcast_to(jnp.arange(pairs, dtype=I32)[:, None] // nc, (pairs, toks))
    digits = jnp.concatenate([flat_index // 32, flat_index % 32, asker], axis=1).astype(BF16)
    digits = jnp.dot(hot.astype(BF16), digits, preferred_element_type=F32)
    digits = digits.astype(I32)
    index = digits[:, :toks] * 32 + digits[:, toks : 2 * toks] + digits[:, 2 * toks :] * 1024
    index = index.reshape(zs, slots * toks // LANES, LANES)
    nt = jnp.concatenate(
        [
            number.astype(F32).reshape(zs, slots),
            teach.reshape(zs, slots),
            jnp.zeros((zs, LANES - 2 * slots), F32),
        ],
        axis=1,
    ).reshape(zs, 1, LANES)

    def dma(*shape):
        return pltpu.SemaphoreType.DMA(shape)

    gq, gp = pl.pallas_call(
        functools.partial(kernel, zs, ys),
        out_shape=(S((nq * toks, width), F32), S((share, width), F32)),
        in_specs=[VMEM] * 5,
        out_specs=(VMEM,) * 2,
        scratch_shapes=[
            V((zs, nq, toks, width), BF16),
            V(index.shape, I32),
            V(nt.shape, F32),
            V((held * patches, width), F32),
            V((ys - 1, rows, width), F32),
            V((rows, width), F32),
            V((X, 2, ys, rows, width), BF16),
            V((slab, zs // 2, LANES), I32),
            V((zs, slots * toks // LANES, LANES), I32),
            V((slab, zs // 2, LANES), F32),
            V((zs, slots * toks // LANES, LANES), F32),
            V((slab, per_page, width), BF16),
            V((slab, per_page, width), BF16),
            V((CAP, zs, LANES), F32),
            V((zs, LANES), F32),
            V((zs, LANES), F32),
            pltpu.SMEM(index.shape, I32),
            V((zs // 8, LANES), F32),
            V((zs - 1, zs // 8, LANES), F32),
            V((X, 2, held * patches, width), F32),
            V((zs, nq * toks, width), F32),
            V((2, half, nq * toks, width), F32),
            V((X, held * patches, width), F32),
            V((X * ys, rows, width), BF16),
            V((X * ys, rows, width), BF16),
            V((ys, rows, width), BF16),
            V((share, width), F32),
            V((near, block, width), F32),
            V((block, width), F32),
            V((zs, 8, width), F32),
            dma(2, half, SUBS), dma(2, half, SUBS),
            dma(ys - 1), dma(ys - 1),
            dma(X * ys - 1), dma(X * ys - 1),
            dma(X * ys), dma(X * ys),
            dma(zs - 1), dma(zs - 1),
            dma(zs - 1), dma(zs - 1),
            pltpu.SemaphoreType.DMA,
            dma(zs - 1), dma(zs - 1),
            dma(2, half, 2), dma(2, half, 2),
            dma(X), dma(X),
            dma(X * ys), dma(X * ys),
            dma(ys - 1), dma(ys - 1),
            dma(near), dma(near),
            dma(block // 8), dma(zs),
            dma(zs), dma(zs),
            dma(near), dma(near),
        ],
        compiler_params=pltpu.CompilerParams(
            collective_id=0, has_side_effects=True, vmem_limit_bytes=56 << 20
        ),
        name="maxsim",
    )(
        page_states.reshape(held * patches, share), projection,
        query_tokens, index, nt,
    )
    return (gq.reshape(nq, toks, width), gp)


def solution(mesh):
    placed = (
        P("pages", None, "queries"),
        P("queries", None),
        P(("pages", "queries"), None, None),
        P(("pages", "queries"), None),
        P(("pages", "queries"), None, None),
        P(("pages", "queries"), None),
        P(),
    )
    return jax.shard_map(
        body,
        mesh=mesh,
        in_specs=placed,
        out_specs=(P(("pages", "queries"), None, None), P("queries", None)),
        check_vma=False,
    )
```

```python
import functools

import jax
import jax.numpy as jnp
from jax import lax
from jax.experimental import pallas as pl
from jax.experimental.pallas import tpu as pltpu
from jax.sharding import PartitionSpec as P

SOFTMAX_HEAT = 0.5
EPSILON = 1e-06
CAP = 2
X = 4
LANES = 128
SUBS = 4
MESH = pl.DeviceIdType.MESH
VMEM = pl.BlockSpec(memory_space=pltpu.VMEM)
F32, BF16, I32 = jnp.float32, jnp.bfloat16, jnp.int32


def unit_rows(values):
    inverse = lax.rsqrt(jnp.sum(values * values, axis=-1, keepdims=True) + EPSILON)
    return (values * inverse, inverse)


def iota(shape, axis):
    return lax.broadcasted_iota(I32, shape, axis)


def remote(src, dst, send, recv, to):
    return pltpu.make_async_remote_copy(
        src_ref=src, dst_ref=dst, send_sem=send, recv_sem=recv, device_id=to, device_id_type=MESH
    )


def prepare_kernel(zs, slab, toks, cand, pidx, logits, pslot, idx, nt):
    queries = cand.shape[0]
    pairs, pages = cand.shape[0] * cand.shape[1], pslot.shape[1]
    nc = cand.shape[1]
    chip = slab // X
    probs = jnp.exp(logits[...])
    probs = probs / jnp.sum(probs, axis=1, keepdims=True)
    repeat = jnp.where(iota((nc, pairs), 1) % nc == iota((nc, pairs), 0), 1.0, 0.0)
    owns = iota((queries, pairs), 1) // nc == iota((queries, pairs), 0)

    def flat(values):
        wide = jnp.dot(
            values, repeat, preferred_element_type=F32, precision=lax.Precision.HIGHEST
        )
        return jnp.sum(jnp.where(owns, wide, 0.0), axis=0, keepdims=True)

    listed = flat(cand[...].astype(F32)).astype(I32) == iota((pages, pairs), 0)
    listed = jnp.where(listed, 1.0, 0.0)
    slot_of = jnp.broadcast_to(pslot[...].astype(F32), (8, pages)).astype(BF16)
    row = jnp.dot(slot_of, listed.astype(BF16), preferred_element_type=F32)[0:1].astype(I32)
    before = jnp.where(iota((pairs, pairs), 0) < iota((pairs, pairs), 1), 1.0, 0.0)
    earlier = jnp.dot(listed.astype(BF16), before.astype(BF16), preferred_element_type=F32)
    arrival = jnp.sum(earlier * listed, axis=0, keepdims=True).astype(I32)
    owner = (row // chip) % zs
    place = row // (chip * zs) * chip + row % chip
    spot = owner * 8 + (place & 7)
    turn = (place >> 3) * CAP + arrival
    patch = pidx[...] + 1
    asker = iota((pairs, toks), 0) // nc
    group = iota((pairs, LANES), 1) // toks
    parts = [
        jnp.concatenate([v.astype(F32)] * (LANES // toks), axis=1)
        for v in (patch >> 5, patch & 31, asker)
    ]
    sums = [jnp.zeros((zs * 8, LANES), F32) for _ in parts]
    for u in range(LANES // toks):
        hot = jnp.where((spot == iota((zs * 8, pairs), 0)) & (turn == u), 1.0, 0.0).astype(BF16)
        for i, v in enumerate(parts):
            v = jnp.where(group == u, v, 0.0).astype(BF16)
            sums[i] = sums[i] + jnp.dot(hot, v, preferred_element_type=F32)
    high, low, asker = (v.astype(I32) for v in sums)
    idx[...] = (high * 32 + low + asker * 1024).reshape(idx.shape)
    turn = arrival * slab + place
    lines = iota((LANES, pairs), 0)
    asker = (iota((LANES, pairs), 1) // nc + 1).astype(F32)
    values = jnp.where(turn == lines, asker, 0.0)
    values = values + jnp.where(turn + CAP * slab == lines, flat(probs), 0.0)
    owned = jnp.where(owner == iota((zs, pairs), 0), 1.0, 0.0)
    tile = lax.dot_general(
        owned, values, (((1,), (1,)), ((), ())),
        preferred_element_type=F32, precision=lax.Precision.HIGHEST,
    )
    tile = tile - jnp.where(iota((zs, LANES), 1) < CAP * slab, 1.0, 0.0)
    for s in range(zs):
        nt[s] = tile[s : s + 1]


def kernel(
    zs, ys,
    states, proj, qraw, idx, nt,
    gq_out, gp_out,
    qall, idxall, ntall, ep, rs, ef, table, kge, kg, wge, wg, picked, qsel, sc, sm, nv, nsm,
    zpart, zseen, ge, gbuf, rbuf, cbuf, sbuf, xbuf, eout, part, abuf, bsrc, bbuf,
    q_s, q_r, e_s, e_r, t_s, t_r, f_s, f_r, i_s, i_r, n_s, n_r, m_s, z_s, z_r,
    g_s, g_r, c_s, c_r, p_s, p_r, y_s, y_r, a_s, a_r, b_s, b_r, o_s, o_r, d_s, d_r,
):
    p = lax.axis_index("pages")
    x, y, z, c = p // (2 * zs), lax.axis_index("queries"), (p // 2) % zs, p % 2

    def at(x_, y_, z_, c_):
        return ((x_ * zs + z_) * 2 + c_, y_)

    def xm(d):
        return (x + d + X) % X

    def ym(d):
        return (y + d + ys) % ys

    def zm(d):
        return (z + d + 2 * zs) % zs

    rows, width = ef.shape
    queries, toks, _ = qraw.shape
    toks_q = queries * toks
    slab = kge.shape[0]
    patches = table.shape[3] * ys // 2
    blocks = ys // 2
    half = zs // 2
    plane = [(dx, dy) for dx in range(X) for dy in range(ys) if dx + dy > 0]
    near_by = [(dx, dc) for dx in range(X) for dc in range(2) if dx + dc > 0]

    barrier = pltpu.get_barrier_semaphore()
    peers = [at(x, y, zm(d), c) for d in range(1, zs)]
    peers += [at(xm(dx), ym(dy), z, c) for dx, dy in plane]
    peers += [at(xm(dx), y, z, 1 - c) for dx in range(X)]
    for to in peers:
        pl.semaphore_signal(barrier, inc=1, device_id=to, device_id_type=MESH)

    qall[z] = unit_rows(qraw[...].astype(F32))[0].astype(BF16)
    ep[...] = jnp.dot(states[...], proj[...], preferred_element_type=F32)
    sm[...] = jnp.zeros_like(sm)

    idxall[z] = idx[z]
    ntall[z] = nt[z]
    pl.semaphore_wait(barrier, len(peers))

    size = queries // SUBS

    def ring(way, s, h, block):
        ref = qall.at[block, pl.ds(h * size, size)]
        k = 0 if way > 0 else 1
        return remote(ref, ref, q_s.at[k, s, h], q_r.at[k, s, h], at(x, y, zm(way), c))

    def ring_parts(way, s):
        if s < half - 1:
            return range(SUBS)
        return range(SUBS // 2) if way > 0 else range(SUBS // 2, SUBS)

    waiting = []

    def start_some(count):
        for _ in range(min(count, len(waiting))):
            waiting.pop(0).start()

    def ring_send(s):
        for h in range(SUBS):
            for way in (1, -1):
                block = zm(-way * s)
                if s > 0:
                    ring(way, s - 1, h, block).wait_recv()
                if h in ring_parts(way, s):
                    ring(way, s, h, block).start()
            start_some(2)

    ring_send(0)
    e_copies = []
    piece = rows // 2
    for hh in range(2):
        for d in range(1, ys):
            src = ep.at[pl.ds(pl.multiple_of(ym(d) * rows + hh * piece, 8), piece)]
            dst = rs.at[d - 1, pl.ds(hh * piece, piece)]
            to = at(x, ym(d), z, c)
            e_copies.append(remote(src, dst, e_s.at[hh, d - 1], e_r.at[hh, d - 1], to))
            if hh == 0:
                e_copies[-1].start()
            else:
                waiting.append(e_copies[-1])
    i_copies = []
    for d in range(1, zs):
        to = at(x, y, zm(d), c)
        for src, dst, s_sem, r_sem in ((idx, idxall, i_s, i_r), (nt, ntall, n_s, n_r)):
            copy = remote(src.at[zm(d)], dst.at[z], s_sem.at[d - 1], r_sem.at[d - 1], to)
            copy.start()
            i_copies.append(copy)
    ring_send(1)

    t_copies = []

    def pass_on(hh, near, far):
        dx, dy = (far, near) if hh == 0 else (near, far)
        i = plane.index((dx, dy))
        if near == 0:
            block, to = (x, y), (xm(dx), ym(dy))
        elif hh == 0:
            block, to = (xm(-dx), y), (x, ym(dy))
        else:
            block, to = (x, ym(-dy)), (xm(dx), y)
        ref = table.at[block[0], c, block[1], pl.ds(hh * piece, piece)]
        to = at(*to, z, c)
        t_copies.append(remote(ref, ref, t_s.at[hh, i], t_r.at[hh, i], to))
        return t_copies[-1]

    def arrived(hh, dx, dy):
        i = plane.index((dx, dy))
        ref = table.at[xm(-dx), c, ym(-dy), pl.ds(hh * piece, piece)]
        remote(ref, ref, t_s.at[hh, i], t_r.at[hh, i], at(xm(dx), ym(dy), z, c)).wait_recv()

    def relay(hh):
        for d in range(1, X):
            arrived(hh, *((d, 0) if hh == 0 else (0, d)))
            for near in range(1, X):
                waiting.append(pass_on(hh, near, d))

    def embed(hh):
        for copy in e_copies[hh * (ys - 1) : (hh + 1) * (ys - 1)]:
            copy.wait_recv()
        cut = pl.ds(hh * piece, piece)
        own = ep[pl.ds(pl.multiple_of(y * rows + hh * piece, 8), piece), :]
        for d in range(1, ys):
            own = own + rs[d - 1, cut, :]
        ef[cut, :] = own
        table[x, c, y, cut, :] = unit_rows(own)[0].astype(BF16)
        for d in range(1, X):
            pass_on(hh, 0, d).start()
        for d in range(1, X):
            waiting.append(pass_on(hh, d, 0))

    embed(0)
    ring_send(2)
    embed(1)
    relay(0)

    def sibling(dx, dy, core):
        i = dx * ys + dy
        ref = table.at[xm(-dx), core, ym(-dy)]
        return remote(ref, ref, f_s.at[i], f_r.at[i], at(x, y, z, 1 - c))

    def forward(dx):
        for dy in range(ys):
            if dx + dy > 0:
                for hh in range(2):
                    if (dy, dx)[hh] > 0:
                        arrived(hh, dx, dy)
            sibling(dx, dy, c).start()

    ring_send(3)
    relay(1)

    ring_send(4)
    ring_send(5)
    forward(0)
    ring_send(6)
    for copy in i_copies:
        copy.wait_recv()
    lane8 = iota((8, LANES), 1)
    for j in range(zs // 2):
        a, b = ((idxall[i] & 1023) - 1 for i in (2 * j, 2 * j + 1))
        kge[0:8, j, :] = jnp.where(lane8 < 64, a, pltpu.roll(b, 64, 1))
        kge[8:16, j, :] = jnp.where(lane8 < 64, pltpu.roll(a, 64, 1), b)
    for s in range(zs):
        nv[s : s + 1, :] = ntall[s]
    lane = iota((zs, LANES), 1)
    number = nv[...]
    valid = (lane < CAP * slab) & (number >= 0)
    teach = pltpu.roll(number, LANES - CAP * slab, 1)
    scalars = pltpu.make_async_copy(idxall, nsm, m_s)
    scalars.start()
    wide = slab * CAP * toks
    lanes = iota((LANES, wide), 1)
    sub = iota((LANES, wide), 0)
    spread = (sub < CAP * slab) & ((sub & (slab - 1)) == (lanes >> 6))
    spread = spread & ((sub >> 4) == ((lanes >> 5) & 1))
    spread = jnp.where(spread, 1.0, 0.0).astype(BF16)
    keys = jnp.dot(
        jnp.where(valid, number, -64.0).astype(BF16), spread, preferred_element_type=F32
    )
    keys = keys.astype(I32) * toks + (iota((zs, wide), 1) & (toks - 1))
    for j in range(wide // LANES):
        kg[:, j, :] = keys[:, j * LANES : (j + 1) * LANES]
    scalars.wait()

    ring_send(7)
    start_some(len(waiting))
    forward(1)
    for way in (1, -1):
        for h in ring_parts(way, half - 1):
            ring(way, half - 1, h, zm(-way * half)).wait_recv()

    def pick_page(m):
        page = table[m // 4, (m // 2) % 2, pl.ds(blocks * (m % 2), blocks)]
        page = page.reshape(patches, width)
        cols = kge[m].T
        ids = iota((LANES, patches), 1).astype(jnp.int16)
        one, none = jnp.ones((), BF16), jnp.zeros((), BF16)
        for g in range(zs // 4):
            hot = jnp.concatenate(
                [
                    jnp.where(cols[:, j : j + 1].astype(jnp.int16) == ids, one, none)
                    for j in (2 * g, 2 * g + 1)
                ],
                axis=0,
            )
            got = jnp.dot(hot, page, preferred_element_type=F32)
            picked[m, g * 256 : (g + 1) * 256, :] = got.astype(BF16)
            for i in range(8):
                s = g * 8 + i
                src, k = s // CAP, s % CAP
                query = qall[src, nsm[src, m % 8, m // 8 * (CAP * toks) + k * toks] >> 10]
                qsel[m, s * toks : (s + 1) * toks, :] = query
                sc[k, src : src + 1, :] = jnp.sum(
                    got[i * toks : (i + 1) * toks] * query.astype(F32), axis=0, keepdims=True
                )
        for k in range(CAP):
            col = jnp.sum(sc[k], axis=1, keepdims=True)
            sm[...] = jnp.where(lane == k * slab + m, col, sm[...])

    for dx in range(X):
        if 0 < dx < X - 1:
            forward(dx + 1)
        for dy in range(ys):
            sibling(dx, dy, 1 - c).wait_recv()

        @pl.loop(0, 4)
        def _(i):
            pick_page(xm(-dx) * 4 + i)

    lifted = jnp.where(valid, jnp.exp(sm[...] / SOFTMAX_HEAT), 0.0)
    wide_sum = jnp.zeros((zs, LANES), F32)
    for n in range(16):
        col = jnp.sum(jnp.where(number == n, lifted, 0.0), axis=1, keepdims=True)
        wide_sum = jnp.where((lane & 15) == n, col, wide_sum)
    diagonal = (lane >> 4) == (iota((zs, LANES), 0) & 7)
    wide_sum = jnp.where(diagonal, wide_sum, 0.0)
    for r in range(zs // 8):
        zpart[r : r + 1, :] = jnp.sum(wide_sum[8 * r : 8 * r + 8], axis=0, keepdims=True)
    z_copies = []
    for d in range(1, zs):
        to = at(x, y, zm(d), c)
        z_copies.append(remote(zpart, zseen.at[d - 1], z_s.at[d - 1], z_r.at[d - 1], to))
        z_copies[-1].start()
    total = zpart[...]
    for d in range(1, zs):
        z_copies[d - 1].wait_recv()
        total = total + zseen[d - 1]
    total = jnp.concatenate(
        [jnp.broadcast_to(total[r : r + 1], (8, LANES)) for r in range(zs // 8)], axis=0
    )
    total = jnp.where(diagonal, total, 0.0)
    denom = jnp.ones((zs, LANES), F32)
    for n in range(16):
        col = jnp.sum(jnp.where((lane & 15) == n, total, 0.0), axis=1, keepdims=True)
        denom = jnp.where(valid & (number == n), col, denom)
    weight = jnp.where(valid, (lifted / denom - teach) / SOFTMAX_HEAT, 0.0)
    wide_w = jnp.dot(weight.astype(BF16), spread, preferred_element_type=F32)
    for j in range(wide // LANES):
        wg[:, j, :] = wide_w[:, j * LANES : (j + 1) * LANES]
    turned = weight.T
    wide_w = jnp.zeros((slab, zs * CAP * toks), F32)
    lanes = iota((zs, zs * CAP * toks), 1)
    sub = iota((zs, zs * CAP * toks), 0)
    for k in range(CAP):
        expand = (sub == (lanes >> 6)) & (((lanes >> 5) & 1) == k)
        expand = jnp.where(expand, 1.0, 0.0).astype(BF16)
        wide_w = wide_w + jnp.dot(
            turned[k * slab : (k + 1) * slab].astype(BF16), expand, preferred_element_type=F32
        )
    for j in range(zs * CAP * toks // LANES):
        wge[:, j, :] = wide_w[:, j * LANES : (j + 1) * LANES]

    def hot_pair(key, scale, a, j, ids):
        return jnp.concatenate(
            [
                jnp.where(
                    key[a, pl.ds(i, 1), :] == ids, scale[a, pl.ds(i, 1), :], 0.0
                ).astype(BF16)
                for i in (2 * j, 2 * j + 1)
            ],
            axis=1,
        )

    def query_block(src):
        out = jnp.zeros((toks_q, width), F32)
        ids = iota((toks_q, LANES), 0)
        per = CAP * toks
        first = pl.multiple_of(src * per, per)
        for j in range(wide // 256):
            rows_of = jnp.concatenate(
                [picked[m, pl.ds(first, per), :] for m in range(4 * j, 4 * j + 4)], axis=0
            )
            out = out + jnp.dot(
                hot_pair(kg, wg, src, j, ids), rows_of, preferred_element_type=F32
            )
        gbuf[src] = out

    def page_block(xx, cc, l):
        m = xx * 4 + cc * 2 + l
        out = jnp.zeros((patches, width), F32)
        ids = iota((patches, LANES), 0)
        for j in range(zs * CAP * toks // 256):
            out = out + jnp.dot(
                hot_pair(kge, wge, m, j, ids), qsel[m, j * 256 : (j + 1) * 256, :],
                preferred_element_type=F32,
            )
        ge[xx, cc, l * patches : (l + 1) * patches, :] = out

    part_rows = toks_q // 2

    def gring(way, s, h, begin=False):
        k = 0 if way > 0 else 1
        cut = pl.ds(h * part_rows, part_rows)
        src = gbuf.at[zm(way * (half - s)), cut] if begin else rbuf.at[k, s - 1, cut]
        return remote(
            src, rbuf.at[k, s, cut], g_s.at[k, s, h], g_r.at[k, s, h], at(x, y, zm(way), c)
        )

    def begins(way, h):
        return 0 if (h == 0) == (way > 0) else 1

    def gstep(s):
        if isinstance(s, int) and s == 0:
            query_block(zm(half))
        else:
            query_block(zm(half - s))
            query_block(zm(s - half))
        for h in range(2):
            for way in (1, -1):
                k = 0 if way > 0 else 1
                begin = isinstance(s, int) and s == begins(way, h)
                if isinstance(s, int) and s < begins(way, h):
                    continue
                if not begin:
                    cut = pl.ds(h * part_rows, part_rows)
                    early = isinstance(s, int) and s - 1 == begins(way, h)
                    gring(way, s - 1, h, early).wait_recv()
                    rbuf[k, s - 1, cut] = rbuf[k, s - 1, cut] + gbuf[zm(way * (half - s)), cut]
                gring(way, s, h, begin).start()

    gstep(0)

    def to_sibling(xx):
        return remote(
            ge.at[xx, 1 - c], cbuf.at[xx], c_s.at[xx], c_r.at[xx], at(x, y, z, 1 - c)
        )

    def to_plane(i, xx, yy):
        return remote(sbuf.at[i], xbuf.at[i], p_s.at[i], p_r.at[i], at(xx, yy, z, c))

    def deliver(d):
        xx = xm(d)
        to_sibling(xx).wait_recv()
        for dy in range(ys):
            cut = pl.ds(pl.multiple_of(ym(dy) * rows, 8), rows)
            i = (d % X) * ys + dy
            sbuf[i] = (ge[xx, c, cut, :] + cbuf[xx, cut, :]).astype(BF16)
            if dy == 0:

                @pl.when(d < X)
                def _():
                    to_plane(i, xx, ym(dy)).start()
            else:
                to_plane(i, xx, ym(dy)).start()

    @pl.loop(1, X + 2)
    def _(d):
        @pl.when(d <= X)
        def _():
            for l in range(2):
                page_block(xm(d), 1 - c, l)
            to_sibling(xm(d)).start()
            for l in range(2):
                page_block(xm(d), c, l)

        @pl.when(d > 1)
        def _():
            deliver(d - 1)

    gstep(1)

    @pl.loop(2, 4)
    def _(s):
        gstep(s)

    cut = pl.ds(pl.multiple_of(y * rows, 8), rows)
    own = ge[x, c, cut, :] + cbuf[x, cut, :]
    for dx, dy in plane:
        i = dx * ys + dy
        to_plane(i, xm(dx), ym(dy)).wait_recv()
        own = own + xbuf[i].astype(F32)
    unit, inverse = unit_rows(ef[...])
    grad = (own - unit * jnp.sum(unit * own, axis=-1, keepdims=True)) * inverse
    eout[y] = grad.astype(BF16)
    y_copies = []
    for d in range(1, ys):
        to = at(x, ym(d), z, c)
        y_copies.append(remote(eout.at[y], eout.at[y], y_s.at[d - 1], y_r.at[d - 1], to))
        y_copies[-1].start()
    gstep(4)
    for copy in y_copies:
        copy.wait_recv()
    part[...] = lax.dot_general(
        eout[...].reshape(ys * rows, width), states[...], (((0,), (0,)), ((), ())),
        preferred_element_type=F32,
    ).T

    share = part.shape[0] // (2 * X)
    owners = share // 8
    near = [at(xm(dx), y, z, (c + dc) % 2) for dx, dc in near_by]

    def block(k):
        return pl.ds(pl.multiple_of(k * share, 8), share)

    def tile(k):
        return pl.ds(pl.multiple_of(k * 8, 8), 8)

    me = x * 2 + c
    a_copies = []
    for i, (dx, dc) in enumerate(near_by):
        k = xm(dx) * 2 + (c + dc) % 2
        a_copies.append(remote(part.at[block(k)], abuf.at[i], a_s.at[i], a_r.at[i], near[i]))
        a_copies[-1].start()
    gstep(5)
    own = part[block(me), :]
    for i, copy in enumerate(a_copies):
        copy.wait_recv()
        own = own + abuf[i]
    bsrc[...] = own

    def b_copy(k, i, to):
        return remote(bsrc.at[tile(k)], bbuf.at[i], b_s.at[k], b_r.at[i], to)

    for k in range(owners):

        @pl.when(z != k)
        def _():
            b_copy(k, z, at(x, y, k, c)).start()

    gstep(6)

    my_tile = pl.ds(pl.multiple_of(me * share + z * 8, 8), 8)

    def o_copy(i, to):
        return remote(gp_out.at[my_tile], gp_out.at[my_tile], o_s.at[i], o_r.at[z], to)

    @pl.when(z < owners)
    def _():
        total = bsrc[tile(z), :]
        for d in range(1, zs):
            i = zm(d)
            b_copy(0, i, at(x, y, i, c)).wait_recv()
            total = total + bbuf[i]
        gp_out[my_tile, :] = total
        for d in range(1, zs):
            o_copy(d - 1, at(x, y, zm(d), c)).start()

    gstep(7)
    query_block(z)

    for k in range(owners):

        @pl.when(z != k)
        def _():
            got = gp_out.at[pl.ds(pl.multiple_of(me * share + k * 8, 8), 8)]
            remote(got, got, o_s.at[0], o_r.at[k], at(x, y, k, c)).wait_recv()

    d_copies = []
    for i in range(len(near_by)):
        ref = gp_out.at[block(me)]
        d_copies.append(remote(ref, ref, d_s.at[i], d_r.at[i], near[i]))
        d_copies[-1].start()
    for way in (1, -1):
        for h in range(2):
            gring(way, half - 1, h).wait_recv()
    unit, inverse = unit_rows(qraw[...].reshape(toks_q, width).astype(F32))
    own = gbuf[z] + rbuf[0, half - 1] + rbuf[1, half - 1]
    gq_out[...] = (own - unit * jnp.sum(unit * own, axis=-1, keepdims=True)) * inverse
    for copy in d_copies:
        copy.wait_recv()

    for s in range(half):
        for way in (1, -1):
            for h in ring_parts(way, s):
                ring(way, s, h, zm(-way * s)).wait_send()
            for h in range(2):
                if s >= begins(way, h):
                    gring(way, s, h, s == begins(way, h)).wait_send()
    for dx in range(X):
        for dy in range(ys):
            sibling(dx, dy, c).wait_send()
            if dx + dy > 0:
                to_plane(dx * ys + dy, xm(dx), ym(dy)).wait_send()
        to_sibling(xm(dx)).wait_send()
    for copy in e_copies + i_copies + t_copies + z_copies + y_copies + a_copies + d_copies:
        copy.wait_send()
    for k in range(owners):

        @pl.when(z != k)
        def _():
            b_copy(k, z, at(x, y, k, c)).wait_send()

    @pl.when(z < owners)
    def _():
        for d in range(1, zs):
            o_copy(d - 1, at(x, y, zm(d), c)).wait_send()


def body(page_states, projection, query_tokens, candidates, patch_index, teacher_logits, page_slot):
    ys = lax.axis_size("queries")
    zs = lax.axis_size("pages") // (2 * X)
    held, patches, share = page_states.shape
    width = projection.shape[1]
    nq, nc, toks = patch_index.shape
    chip = 2 * held
    slab = X * chip
    slots = slab * CAP
    rows = held * patches // ys
    half = zs // 2
    per_page = zs * CAP * toks
    near = 2 * X - 1
    block = share // (2 * X)
    S = jax.ShapeDtypeStruct
    V = pltpu.VMEM

    def dma(*shape):
        return pltpu.SemaphoreType.DMA(shape)

    index, nt = pl.pallas_call(
        functools.partial(prepare_kernel, zs, slab, toks),
        out_shape=(S((zs, 8, LANES), I32), S((zs, 1, LANES), F32)),
        in_specs=[VMEM] * 4,
        out_specs=(VMEM,) * 2,
        name="prepare",
    )(
        candidates, patch_index.reshape(nq * nc, toks), teacher_logits, page_slot.reshape(1, -1)
    )
    gq, gp = pl.pallas_call(
        functools.partial(kernel, zs, ys),
        out_shape=(S((nq * toks, width), F32), S((share, width), F32)),
        in_specs=[VMEM] * 5,
        out_specs=(VMEM,) * 2,
        scratch_shapes=[
            V((zs, nq, toks, width), BF16),
            V((zs, 8, LANES), I32),
            V((zs, 1, LANES), F32),
            V((held * patches, width), F32),
            V((ys - 1, rows, width), F32),
            V((rows, width), F32),
            V((X, 2, ys, rows, width), BF16),
            V((slab, zs // 2, LANES), I32),
            V((zs, slots * toks // LANES, LANES), I32),
            V((slab, zs // 2, LANES), F32),
            V((zs, slots * toks // LANES, LANES), F32),
            V((slab, per_page, width), BF16),
            V((slab, per_page, width), BF16),
            V((CAP, zs, LANES), F32),
            V((zs, LANES), F32),
            V((zs, LANES), F32),
            pltpu.SMEM((zs, 8, LANES), I32),
            V((zs // 8, LANES), F32),
            V((zs - 1, zs // 8, LANES), F32),
            V((X, 2, held * patches, width), F32),
            V((zs, nq * toks, width), F32),
            V((2, half, nq * toks, width), F32),
            V((X, held * patches, width), F32),
            V((X * ys, rows, width), BF16),
            V((X * ys, rows, width), BF16),
            V((ys, rows, width), BF16),
            V((share, width), F32),
            V((near, block, width), F32),
            V((block, width), F32),
            V((zs, 8, width), F32),
            dma(2, half, SUBS), dma(2, half, SUBS),
            dma(2, ys - 1), dma(2, ys - 1),
            dma(2, X * ys - 1), dma(2, X * ys - 1),
            dma(X * ys), dma(X * ys),
            dma(zs - 1), dma(zs - 1),
            dma(zs - 1), dma(zs - 1),
            pltpu.SemaphoreType.DMA,
            dma(zs - 1), dma(zs - 1),
            dma(2, half, 2), dma(2, half, 2),
            dma(X), dma(X),
            dma(X * ys), dma(X * ys),
            dma(ys - 1), dma(ys - 1),
            dma(near), dma(near),
            dma(block // 8), dma(zs),
            dma(zs), dma(zs),
            dma(near), dma(near),
        ],
        compiler_params=pltpu.CompilerParams(
            collective_id=0, has_side_effects=True, vmem_limit_bytes=56 << 20
        ),
        name="maxsim",
    )(
        page_states.reshape(held * patches, share), projection,
        query_tokens, index, nt,
    )
    return (gq.reshape(nq, toks, width), gp)


def solution(mesh):
    placed = (
        P("pages", None, "queries"),
        P("queries", None),
        P(("pages", "queries"), None, None),
        P(("pages", "queries"), None),
        P(("pages", "queries"), None, None),
        P(("pages", "queries"), None),
        P(),
    )
    return jax.shard_map(
        body,
        mesh=mesh,
        in_specs=placed,
        out_specs=(P(("pages", "queries"), None, None), P("queries", None)),
        check_vma=False,
    )
```

```python
import functools

import jax
import jax.numpy as jnp
from jax import lax
from jax.experimental import pallas as pl
from jax.experimental.pallas import tpu as pltpu
from jax.sharding import PartitionSpec as P

SOFTMAX_HEAT = 0.5
EPSILON = 1e-06
CAP = 2
X = 4
LANES = 128
SUBS = 4
MESH = pl.DeviceIdType.MESH
VMEM = pl.BlockSpec(memory_space=pltpu.VMEM)
F32, BF16, I32 = jnp.float32, jnp.bfloat16, jnp.int32


def unit_rows(values):
    inverse = lax.rsqrt(jnp.sum(values * values, axis=-1, keepdims=True) + EPSILON)
    return (values * inverse, inverse)


def iota(shape, axis):
    return lax.broadcasted_iota(I32, shape, axis)


def remote(src, dst, send, recv, to):
    return pltpu.make_async_remote_copy(
        src_ref=src, dst_ref=dst, send_sem=send, recv_sem=recv, device_id=to, device_id_type=MESH
    )


def prepare_kernel(zs, slab, toks, cand, pidx, logits, pslot, idx, nt):
    queries = cand.shape[0]
    pairs, pages = cand.shape[0] * cand.shape[1], pslot.shape[1]
    nc = cand.shape[1]
    chip = slab // X
    probs = jnp.exp(logits[...])
    probs = probs / jnp.sum(probs, axis=1, keepdims=True)
    repeat = jnp.where(iota((nc, pairs), 1) % nc == iota((nc, pairs), 0), 1.0, 0.0)
    owns = iota((queries, pairs), 1) // nc == iota((queries, pairs), 0)

    def flat(values):
        wide = jnp.dot(
            values, repeat, preferred_element_type=F32, precision=lax.Precision.HIGHEST
        )
        return jnp.sum(jnp.where(owns, wide, 0.0), axis=0, keepdims=True)

    listed = flat(cand[...].astype(F32)).astype(I32) == iota((pages, pairs), 0)
    listed = jnp.where(listed, 1.0, 0.0)
    slot_of = jnp.broadcast_to(pslot[...].astype(F32), (8, pages)).astype(BF16)
    row = jnp.dot(slot_of, listed.astype(BF16), preferred_element_type=F32)[0:1].astype(I32)
    before = jnp.where(iota((pairs, pairs), 0) < iota((pairs, pairs), 1), 1.0, 0.0)
    earlier = jnp.dot(listed.astype(BF16), before.astype(BF16), preferred_element_type=F32)
    arrival = jnp.sum(earlier * listed, axis=0, keepdims=True).astype(I32)
    owner = (row // chip) % zs
    place = row // (chip * zs) * chip + row % chip
    spot = owner * 8 + (place & 7)
    turn = (place >> 3) * CAP + arrival
    patch = pidx[...] + 1
    asker = iota((pairs, toks), 0) // nc
    group = iota((pairs, LANES), 1) // toks
    parts = [
        jnp.concatenate([v.astype(F32)] * (LANES // toks), axis=1)
        for v in (patch >> 5, patch & 31, asker)
    ]
    sums = [jnp.zeros((zs * 8, LANES), F32) for _ in parts]
    for u in range(LANES // toks):
        hot = jnp.where((spot == iota((zs * 8, pairs), 0)) & (turn == u), 1.0, 0.0).astype(BF16)
        for i, v in enumerate(parts):
            v = jnp.where(group == u, v, 0.0).astype(BF16)
            sums[i] = sums[i] + jnp.dot(hot, v, preferred_element_type=F32)
    high, low, asker = (v.astype(I32) for v in sums)
    idx[...] = (high * 32 + low + asker * 1024).reshape(idx.shape)
    turn = arrival * slab + place
    lines = iota((LANES, pairs), 0)
    asker = (iota((LANES, pairs), 1) // nc + 1).astype(F32)
    values = jnp.where(turn == lines, asker, 0.0)
    values = values + jnp.where(turn + CAP * slab == lines, flat(probs), 0.0)
    owned = jnp.where(owner == iota((zs, pairs), 0), 1.0, 0.0)
    tile = lax.dot_general(
        owned, values, (((1,), (1,)), ((), ())),
        preferred_element_type=F32, precision=lax.Precision.HIGHEST,
    )
    tile = tile - jnp.where(iota((zs, LANES), 1) < CAP * slab, 1.0, 0.0)
    for s in range(zs):
        nt[s] = tile[s : s + 1]


def kernel(
    zs, ys,
    states, proj, qraw, idx, nt,
    gq_out, gp_out,
    qall, idxall, ntall, ep, rs, ef, table, kge, kg, wge, wg, picked, qsel, sc, sm, nv, nsm,
    zpart, zseen, ge, gbuf, rbuf, cbuf, sbuf, xbuf, eout, part, abuf, bsrc, bbuf,
    q_s, q_r, e_s, e_r, t_s, t_r, f_s, f_r, i_s, i_r, n_s, n_r, m_s, z_s, z_r,
    g_s, g_r, c_s, c_r, p_s, p_r, y_s, y_r, a_s, a_r, b_s, b_r, o_s, o_r, d_s, d_r,
):
    p = lax.axis_index("pages")
    x, y, z, c = p // (2 * zs), lax.axis_index("queries"), (p // 2) % zs, p % 2

    def at(x_, y_, z_, c_):
        return ((x_ * zs + z_) * 2 + c_, y_)

    def xm(d):
        return (x + d + X) % X

    def ym(d):
        return (y + d + ys) % ys

    def zm(d):
        return (z + d + 2 * zs) % zs

    rows, width = ef.shape
    queries, toks, _ = qraw.shape
    toks_q = queries * toks
    slab = kge.shape[0]
    patches = table.shape[3] * ys // 2
    blocks = ys // 2
    half = zs // 2
    plane = [(dx, dy) for dx in range(X) for dy in range(ys) if dx + dy > 0]
    near_by = [(dx, dc) for dx in range(X) for dc in range(2) if dx + dc > 0]

    barrier = pltpu.get_barrier_semaphore()
    peers = [at(x, y, zm(d), c) for d in range(1, zs)]
    peers += [at(xm(dx), ym(dy), z, c) for dx, dy in plane]
    peers += [at(xm(dx), y, z, 1 - c) for dx in range(X)]
    for to in peers:
        pl.semaphore_signal(barrier, inc=1, device_id=to, device_id_type=MESH)

    qall[z] = unit_rows(qraw[...].astype(F32))[0].astype(BF16)
    ep[...] = jnp.dot(states[...], proj[...], preferred_element_type=F32)
    sm[...] = jnp.zeros_like(sm)

    idxall[z] = idx[z]
    ntall[z] = nt[z]
    pl.semaphore_wait(barrier, len(peers))

    size = queries // SUBS

    def ring(way, s, h, block):
        ref = qall.at[block, pl.ds(h * size, size)]
        k = 0 if way > 0 else 1
        return remote(ref, ref, q_s.at[k, s, h], q_r.at[k, s, h], at(x, y, zm(way), c))

    def ring_parts(way, s):
        if s < half - 1:
            return range(SUBS)
        return range(SUBS // 2) if way > 0 else range(SUBS // 2, SUBS)

    waiting = []

    def start_some(count):
        for _ in range(min(count, len(waiting))):
            waiting.pop(0).start()

    def ring_send(s):
        for h in range(SUBS):
            for way in (1, -1):
                block = zm(-way * s)
                if s > 0:
                    ring(way, s - 1, h, block).wait_recv()
                if h in ring_parts(way, s):
                    ring(way, s, h, block).start()
            start_some(2)

    ring_send(0)
    e_copies = []
    piece = rows // 2
    for hh in range(2):
        for d in range(1, ys):
            src = ep.at[pl.ds(pl.multiple_of(ym(d) * rows + hh * piece, 8), piece)]
            dst = rs.at[d - 1, pl.ds(hh * piece, piece)]
            to = at(x, ym(d), z, c)
            e_copies.append(remote(src, dst, e_s.at[hh, d - 1], e_r.at[hh, d - 1], to))
            if hh == 0:
                e_copies[-1].start()
            else:
                waiting.append(e_copies[-1])
    i_copies = []
    for d in range(1, zs):
        to = at(x, y, zm(d), c)
        for src, dst, s_sem, r_sem in ((idx, idxall, i_s, i_r), (nt, ntall, n_s, n_r)):
            copy = remote(src.at[zm(d)], dst.at[z], s_sem.at[d - 1], r_sem.at[d - 1], to)
            copy.start()
            i_copies.append(copy)
    ring_send(1)

    t_copies = []

    def pass_on(hh, near, far):
        dx, dy = (far, near) if hh == 0 else (near, far)
        i = plane.index((dx, dy))
        if near == 0:
            block, to = (x, y), (xm(dx), ym(dy))
        elif hh == 0:
            block, to = (xm(-dx), y), (x, ym(dy))
        else:
            block, to = (x, ym(-dy)), (xm(dx), y)
        ref = table.at[block[0], c, block[1], pl.ds(hh * piece, piece)]
        to = at(*to, z, c)
        t_copies.append(remote(ref, ref, t_s.at[hh, i], t_r.at[hh, i], to))
        return t_copies[-1]

    def arrived(hh, dx, dy):
        i = plane.index((dx, dy))
        ref = table.at[xm(-dx), c, ym(-dy), pl.ds(hh * piece, piece)]
        remote(ref, ref, t_s.at[hh, i], t_r.at[hh, i], at(xm(dx), ym(dy), z, c)).wait_recv()

    def relay(hh):
        for d in range(1, X):
            arrived(hh, *((d, 0) if hh == 0 else (0, d)))
            for near in range(1, X):
                waiting.append(pass_on(hh, near, d))

    def embed(hh):
        for copy in e_copies[hh * (ys - 1) : (hh + 1) * (ys - 1)]:
            copy.wait_recv()
        cut = pl.ds(hh * piece, piece)
        own = ep[pl.ds(pl.multiple_of(y * rows + hh * piece, 8), piece), :]
        for d in range(1, ys):
            own = own + rs[d - 1, cut, :]
        ef[cut, :] = own
        table[x, c, y, cut, :] = unit_rows(own)[0].astype(BF16)
        for d in range(1, X):
            pass_on(hh, 0, d).start()
        for d in range(1, X):
            waiting.append(pass_on(hh, d, 0))

    embed(0)
    ring_send(2)
    embed(1)
    relay(0)

    def sibling(dx, dy, core):
        i = dx * ys + dy
        ref = table.at[xm(-dx), core, ym(-dy)]
        return remote(ref, ref, f_s.at[i], f_r.at[i], at(x, y, z, 1 - c))

    def forward(dx):
        for dy in range(ys):
            if dx + dy > 0:
                for hh in range(2):
                    if (dy, dx)[hh] > 0:
                        arrived(hh, dx, dy)
            sibling(dx, dy, c).start()

    ring_send(3)
    relay(1)

    ring_send(4)
    ring_send(5)
    forward(0)
    ring_send(6)
    for copy in i_copies:
        copy.wait_recv()
    lane8 = iota((8, LANES), 1)
    for j in range(zs // 2):
        a, b = ((idxall[i] & 1023) - 1 for i in (2 * j, 2 * j + 1))
        kge[0:8, j, :] = jnp.where(lane8 < 64, a, pltpu.roll(b, 64, 1))
        kge[8:16, j, :] = jnp.where(lane8 < 64, pltpu.roll(a, 64, 1), b)
    for s in range(zs):
        nv[s : s + 1, :] = ntall[s]
    lane = iota((zs, LANES), 1)
    number = nv[...]
    valid = (lane < CAP * slab) & (number >= 0)
    teach = pltpu.roll(number, LANES - CAP * slab, 1)
    scalars = pltpu.make_async_copy(idxall, nsm, m_s)
    scalars.start()
    wide = slab * CAP * toks
    lanes = iota((LANES, wide), 1)
    sub = iota((LANES, wide), 0)
    spread = (sub < CAP * slab) & ((sub & (slab - 1)) == (lanes >> 6))
    spread = spread & ((sub >> 4) == ((lanes >> 5) & 1))
    spread = jnp.where(spread, 1.0, 0.0).astype(BF16)
    keys = jnp.dot(
        jnp.where(valid, number, -64.0).astype(BF16), spread, preferred_element_type=F32
    )
    keys = keys.astype(I32) * toks + (iota((zs, wide), 1) & (toks - 1))
    for j in range(wide // LANES):
        kg[:, j, :] = keys[:, j * LANES : (j + 1) * LANES]
    scalars.wait()

    ring_send(7)
    start_some(len(waiting))
    forward(1)
    for way in (1, -1):
        for h in ring_parts(way, half - 1):
            ring(way, half - 1, h, zm(-way * half)).wait_recv()

    def pick_page(m):
        page = table[m // 4, (m // 2) % 2, pl.ds(blocks * (m % 2), blocks)]
        page = page.reshape(patches, width)
        cols = kge[m].T
        ids = iota((LANES, patches), 1).astype(jnp.int16)
        one, none = jnp.ones((), BF16), jnp.zeros((), BF16)
        for g in range(zs // 4):
            hot = jnp.concatenate(
                [
                    jnp.where(cols[:, j : j + 1].astype(jnp.int16) == ids, one, none)
                    for j in (2 * g, 2 * g + 1)
                ],
                axis=0,
            )
            got = jnp.dot(hot, page, preferred_element_type=F32)
            picked[m, g * 256 : (g + 1) * 256, :] = got.astype(BF16)
            for i in range(8):
                s = g * 8 + i
                src, k = s // CAP, s % CAP
                query = qall[src, nsm[src, m % 8, m // 8 * (CAP * toks) + k * toks] >> 10]
                qsel[m, s * toks : (s + 1) * toks, :] = query
                sc[k, src : src + 1, :] = jnp.sum(
                    got[i * toks : (i + 1) * toks] * query.astype(F32), axis=0, keepdims=True
                )
        for k in range(CAP):
            col = jnp.sum(sc[k], axis=1, keepdims=True)
            sm[...] = jnp.where(lane == k * slab + m, col, sm[...])

    for dx in range(X):
        if 0 < dx < X - 1:
            forward(dx + 1)
        for dy in range(ys):
            sibling(dx, dy, 1 - c).wait_recv()

        @pl.loop(0, 4)
        def _(i):
            pick_page(xm(-dx) * 4 + i)

    lifted = jnp.where(valid, jnp.exp(sm[...] / SOFTMAX_HEAT), 0.0)
    wide_sum = jnp.zeros((zs, LANES), F32)
    for n in range(16):
        col = jnp.sum(jnp.where(number == n, lifted, 0.0), axis=1, keepdims=True)
        wide_sum = jnp.where((lane & 15) == n, col, wide_sum)
    diagonal = (lane >> 4) == (iota((zs, LANES), 0) & 7)
    wide_sum = jnp.where(diagonal, wide_sum, 0.0)
    for r in range(zs // 8):
        zpart[r : r + 1, :] = jnp.sum(wide_sum[8 * r : 8 * r + 8], axis=0, keepdims=True)
    z_copies = []
    for d in range(1, zs):
        to = at(x, y, zm(d), c)
        z_copies.append(remote(zpart, zseen.at[d - 1], z_s.at[d - 1], z_r.at[d - 1], to))
        z_copies[-1].start()
    total = zpart[...]
    for d in range(1, zs):
        z_copies[d - 1].wait_recv()
        total = total + zseen[d - 1]
    total = jnp.concatenate(
        [jnp.broadcast_to(total[r : r + 1], (8, LANES)) for r in range(zs // 8)], axis=0
    )
    total = jnp.where(diagonal, total, 0.0)
    denom = jnp.ones((zs, LANES), F32)
    for n in range(16):
        col = jnp.sum(jnp.where((lane & 15) == n, total, 0.0), axis=1, keepdims=True)
        denom = jnp.where(valid & (number == n), col, denom)
    weight = jnp.where(valid, (lifted / denom - teach) / SOFTMAX_HEAT, 0.0)
    wide_w = jnp.dot(weight.astype(BF16), spread, preferred_element_type=F32)
    for j in range(wide // LANES):
        wg[:, j, :] = wide_w[:, j * LANES : (j + 1) * LANES]
    turned = weight.T
    wide_w = jnp.zeros((slab, zs * CAP * toks), F32)
    lanes = iota((zs, zs * CAP * toks), 1)
    sub = iota((zs, zs * CAP * toks), 0)
    for k in range(CAP):
        expand = (sub == (lanes >> 6)) & (((lanes >> 5) & 1) == k)
        expand = jnp.where(expand, 1.0, 0.0).astype(BF16)
        wide_w = wide_w + jnp.dot(
            turned[k * slab : (k + 1) * slab].astype(BF16), expand, preferred_element_type=F32
        )
    for j in range(zs * CAP * toks // LANES):
        wge[:, j, :] = wide_w[:, j * LANES : (j + 1) * LANES]

    def hot_pair(key, scale, a, j, ids):
        return jnp.concatenate(
            [
                jnp.where(
                    key[a, pl.ds(i, 1), :] == ids, scale[a, pl.ds(i, 1), :], 0.0
                ).astype(BF16)
                for i in (2 * j, 2 * j + 1)
            ],
            axis=1,
        )

    def query_block(src):
        out = jnp.zeros((toks_q, width), F32)
        ids = iota((toks_q, LANES), 0)
        per = CAP * toks
        first = pl.multiple_of(src * per, per)
        for j in range(wide // 256):
            rows_of = jnp.concatenate(
                [picked[m, pl.ds(first, per), :] for m in range(4 * j, 4 * j + 4)], axis=0
            )
            out = out + jnp.dot(
                hot_pair(kg, wg, src, j, ids), rows_of, preferred_element_type=F32
            )
        gbuf[src] = out

    def page_block(xx, cc, l):
        m = xx * 4 + cc * 2 + l
        out = jnp.zeros((patches, width), F32)
        ids = iota((patches, LANES), 0)
        for j in range(zs * CAP * toks // 256):
            out = out + jnp.dot(
                hot_pair(kge, wge, m, j, ids), qsel[m, j * 256 : (j + 1) * 256, :],
                preferred_element_type=F32,
            )
        ge[xx, cc, l * patches : (l + 1) * patches, :] = out

    part_rows = toks_q // 2

    def gring(way, s, h, begin=False):
        k = 0 if way > 0 else 1
        cut = pl.ds(h * part_rows, part_rows)
        src = gbuf.at[zm(way * (half - s)), cut] if begin else rbuf.at[k, s - 1, cut]
        return remote(
            src, rbuf.at[k, s, cut], g_s.at[k, s, h], g_r.at[k, s, h], at(x, y, zm(way), c)
        )

    def begins(way, h):
        return 0 if (h == 0) == (way > 0) else 1

    def gstep(s):
        if isinstance(s, int) and s == 0:
            query_block(zm(half))
        else:
            query_block(zm(half - s))
            query_block(zm(s - half))
        for h in range(2):
            for way in (1, -1):
                k = 0 if way > 0 else 1
                begin = isinstance(s, int) and s == begins(way, h)
                if isinstance(s, int) and s < begins(way, h):
                    continue
                if not begin:
                    cut = pl.ds(h * part_rows, part_rows)
                    early = isinstance(s, int) and s - 1 == begins(way, h)
                    gring(way, s - 1, h, early).wait_recv()
                    rbuf[k, s - 1, cut] = rbuf[k, s - 1, cut] + gbuf[zm(way * (half - s)), cut]
                gring(way, s, h, begin).start()

    gstep(0)

    def to_sibling(xx):
        return remote(
            ge.at[xx, 1 - c], cbuf.at[xx], c_s.at[xx], c_r.at[xx], at(x, y, z, 1 - c)
        )

    def to_plane(i, xx, yy):
        return remote(sbuf.at[i], xbuf.at[i], p_s.at[i], p_r.at[i], at(xx, yy, z, c))

    def deliver(d):
        xx = xm(d)
        to_sibling(xx).wait_recv()
        for dy in range(ys):
            cut = pl.ds(pl.multiple_of(ym(dy) * rows, 8), rows)
            i = (d % X) * ys + dy
            sbuf[i] = (ge[xx, c, cut, :] + cbuf[xx, cut, :]).astype(BF16)
            if dy == 0:

                @pl.when(d < X)
                def _():
                    to_plane(i, xx, ym(dy)).start()
            else:
                to_plane(i, xx, ym(dy)).start()

    @pl.loop(1, X + 2)
    def _(d):
        @pl.when(d <= X)
        def _():
            for l in range(2):
                page_block(xm(d), 1 - c, l)
            to_sibling(xm(d)).start()
            for l in range(2):
                page_block(xm(d), c, l)

        @pl.when(d > 1)
        def _():
            deliver(d - 1)

    gstep(1)

    @pl.loop(2, 4)
    def _(s):
        gstep(s)

    cut = pl.ds(pl.multiple_of(y * rows, 8), rows)
    own = ge[x, c, cut, :] + cbuf[x, cut, :]
    for dx, dy in plane:
        i = dx * ys + dy
        to_plane(i, xm(dx), ym(dy)).wait_recv()
        own = own + xbuf[i].astype(F32)
    unit, inverse = unit_rows(ef[...])
    grad = (own - unit * jnp.sum(unit * own, axis=-1, keepdims=True)) * inverse
    eout[y] = grad.astype(BF16)
    y_copies = []
    for d in range(1, ys):
        to = at(x, ym(d), z, c)
        y_copies.append(remote(eout.at[y], eout.at[y], y_s.at[d - 1], y_r.at[d - 1], to))
        y_copies[-1].start()
    gstep(4)
    for copy in y_copies:
        copy.wait_recv()
    part[...] = lax.dot_general(
        eout[...].reshape(ys * rows, width), states[...], (((0,), (0,)), ((), ())),
        preferred_element_type=F32,
    ).T

    share = part.shape[0] // (2 * X)
    owners = share // 8
    near = [at(xm(dx), y, z, (c + dc) % 2) for dx, dc in near_by]

    def block(k):
        return pl.ds(pl.multiple_of(k * share, 8), share)

    def tile(k):
        return pl.ds(pl.multiple_of(k * 8, 8), 8)

    me = x * 2 + c
    a_copies = []
    for i, (dx, dc) in enumerate(near_by):
        k = xm(dx) * 2 + (c + dc) % 2
        a_copies.append(remote(part.at[block(k)], abuf.at[i], a_s.at[i], a_r.at[i], near[i]))
        a_copies[-1].start()
    gstep(5)
    own = part[block(me), :]
    for i, copy in enumerate(a_copies):
        copy.wait_recv()
        own = own + abuf[i]
    bsrc[...] = own

    def b_copy(k, i, to):
        return remote(bsrc.at[tile(k)], bbuf.at[i], b_s.at[k], b_r.at[i], to)

    for k in range(owners):

        @pl.when(z != k)
        def _():
            b_copy(k, z, at(x, y, k, c)).start()

    gstep(6)

    my_tile = pl.ds(pl.multiple_of(me * share + z * 8, 8), 8)

    def o_copy(i, to):
        return remote(gp_out.at[my_tile], gp_out.at[my_tile], o_s.at[i], o_r.at[z], to)

    @pl.when(z < owners)
    def _():
        total = bsrc[tile(z), :]
        for d in range(1, zs):
            i = zm(d)
            b_copy(0, i, at(x, y, i, c)).wait_recv()
            total = total + bbuf[i]
        gp_out[my_tile, :] = total
        for d in range(1, zs):
            o_copy(d - 1, at(x, y, zm(d), c)).start()

    gstep(7)
    query_block(z)

    for k in range(owners):

        @pl.when(z != k)
        def _():
            got = gp_out.at[pl.ds(pl.multiple_of(me * share + k * 8, 8), 8)]
            remote(got, got, o_s.at[0], o_r.at[k], at(x, y, k, c)).wait_recv()

    d_copies = []
    for i in range(len(near_by)):
        ref = gp_out.at[block(me)]
        d_copies.append(remote(ref, ref, d_s.at[i], d_r.at[i], near[i]))
        d_copies[-1].start()
    for way in (1, -1):
        for h in range(2):
            gring(way, half - 1, h).wait_recv()
    unit, inverse = unit_rows(qraw[...].reshape(toks_q, width).astype(F32))
    own = gbuf[z] + rbuf[0, half - 1] + rbuf[1, half - 1]
    gq_out[...] = (own - unit * jnp.sum(unit * own, axis=-1, keepdims=True)) * inverse
    for copy in d_copies:
        copy.wait_recv()

    for s in range(half):
        for way in (1, -1):
            for h in ring_parts(way, s):
                ring(way, s, h, zm(-way * s)).wait_send()
            for h in range(2):
                if s >= begins(way, h):
                    gring(way, s, h, s == begins(way, h)).wait_send()
    for dx in range(X):
        for dy in range(ys):
            sibling(dx, dy, c).wait_send()
            if dx + dy > 0:
                to_plane(dx * ys + dy, xm(dx), ym(dy)).wait_send()
        to_sibling(xm(dx)).wait_send()
    for copy in e_copies + i_copies + t_copies + z_copies + y_copies + a_copies + d_copies:
        copy.wait_send()
    for k in range(owners):

        @pl.when(z != k)
        def _():
            b_copy(k, z, at(x, y, k, c)).wait_send()

    @pl.when(z < owners)
    def _():
        for d in range(1, zs):
            o_copy(d - 1, at(x, y, zm(d), c)).wait_send()


def store_kernel(a, b, a_out, b_out):
    a_out[...] = a[...]
    b_out[...] = b[...]


def body(page_states, projection, query_tokens, candidates, patch_index, teacher_logits, page_slot):
    ys = lax.axis_size("queries")
    zs = lax.axis_size("pages") // (2 * X)
    held, patches, share = page_states.shape
    width = projection.shape[1]
    nq, nc, toks = patch_index.shape
    chip = 2 * held
    slab = X * chip
    slots = slab * CAP
    rows = held * patches // ys
    half = zs // 2
    per_page = zs * CAP * toks
    near = 2 * X - 1
    block = share // (2 * X)
    S = jax.ShapeDtypeStruct
    V = pltpu.VMEM

    def dma(*shape):
        return pltpu.SemaphoreType.DMA(shape)

    index, nt = pl.pallas_call(
        functools.partial(prepare_kernel, zs, slab, toks),
        out_shape=(S((zs, 8, LANES), I32), S((zs, 1, LANES), F32)),
        in_specs=[VMEM] * 4,
        out_specs=(VMEM,) * 2,
        name="prepare",
    )(
        candidates, patch_index.reshape(nq * nc, toks), teacher_logits, page_slot.reshape(1, -1)
    )
    gq, gp = pl.pallas_call(
        functools.partial(kernel, zs, ys),
        out_shape=(S((nq * toks, width), F32), S((share, width), F32)),
        in_specs=[VMEM] * 5,
        out_specs=(VMEM,) * 2,
        scratch_shapes=[
            V((zs, nq, toks, width), BF16),
            V((zs, 8, LANES), I32),
            V((zs, 1, LANES), F32),
            V((held * patches, width), F32),
            V((ys - 1, rows, width), F32),
            V((rows, width), F32),
            V((X, 2, ys, rows, width), BF16),
            V((slab, zs // 2, LANES), I32),
            V((zs, slots * toks // LANES, LANES), I32),
            V((slab, zs // 2, LANES), F32),
            V((zs, slots * toks // LANES, LANES), F32),
            V((slab, per_page, width), BF16),
            V((slab, per_page, width), BF16),
            V((CAP, zs, LANES), F32),
            V((zs, LANES), F32),
            V((zs, LANES), F32),
            pltpu.SMEM((zs, 8, LANES), I32),
            V((zs // 8, LANES), F32),
            V((zs - 1, zs // 8, LANES), F32),
            V((X, 2, held * patches, width), F32),
            V((zs, nq * toks, width), F32),
            V((2, half, nq * toks, width), F32),
            V((X, held * patches, width), F32),
            V((X * ys, rows, width), BF16),
            V((X * ys, rows, width), BF16),
            V((ys, rows, width), BF16),
            V((share, width), F32),
            V((near, block, width), F32),
            V((block, width), F32),
            V((zs, 8, width), F32),
            dma(2, half, SUBS), dma(2, half, SUBS),
            dma(2, ys - 1), dma(2, ys - 1),
            dma(2, X * ys - 1), dma(2, X * ys - 1),
            dma(X * ys), dma(X * ys),
            dma(zs - 1), dma(zs - 1),
            dma(zs - 1), dma(zs - 1),
            pltpu.SemaphoreType.DMA,
            dma(zs - 1), dma(zs - 1),
            dma(2, half, 2), dma(2, half, 2),
            dma(X), dma(X),
            dma(X * ys), dma(X * ys),
            dma(ys - 1), dma(ys - 1),
            dma(near), dma(near),
            dma(block // 8), dma(zs),
            dma(zs), dma(zs),
            dma(near), dma(near),
        ],
        compiler_params=pltpu.CompilerParams(
            collective_id=0, has_side_effects=True, vmem_limit_bytes=56 << 20
        ),
        name="maxsim",
    )(
        page_states.reshape(held * patches, share), projection,
        query_tokens, index, nt,
    )
    gq, gp = pl.pallas_call(
        store_kernel,
        out_shape=(S(gq.shape, F32), S(gp.shape, F32)),
        in_specs=[VMEM] * 2,
        out_specs=(VMEM,) * 2,
        name="store",
    )(gq, gp)
    return (gq.reshape(nq, toks, width), gp)


def solution(mesh):
    placed = (
        P("pages", None, "queries"),
        P("queries", None),
        P(("pages", "queries"), None, None),
        P(("pages", "queries"), None),
        P(("pages", "queries"), None, None),
        P(("pages", "queries"), None),
        P(),
    )
    return jax.shard_map(
        body,
        mesh=mesh,
        in_specs=placed,
        out_specs=(P(("pages", "queries"), None, None), P("queries", None)),
        check_vma=False,
    )
```
